32 devices in a mesh: seq: 16 (over z, x, core), head: 2 (over y).
Axes of the slice: x: 2, y: 2, z: 4, core: 2. Of those that a mesh axis runs over, the one named last changes fastest.
Arguments:
- queries: bfloat16 [16, 4096, 128], P('head', 'seq'), may hold values from -1.75 to 1.75
- key_rows: bfloat16 [16, 4096, 128], P('head', 'seq'), may hold values from -1.75 to 1.75
- value_rows: bfloat16 [16, 4096, 128], P('head', 'seq'), may hold values from -1.75 to 1.75
- grad_out: bfloat16 [16, 4096, 128], P('head', 'seq'), may hold values from -1.75 to 1.75
Outputs:
- grad_query: bfloat16 [16, 4096, 128], P('head', 'seq')
- grad_key: bfloat16 [16, 4096, 128], P('head', 'seq')
- grad_value: bfloat16 [16, 4096, 128], P('head', 'seq')
The draws below stay inside these ranges and needn't reach their ends.
All inputs are finite; a program needn't handle non-finite values.
Results may differ from the reference program's by a relative error of at most 0.0049.
Values sent between devices are 32-bit elements; how exact they have to be, the bound alone decides.
No kernel may reach another device: no remote copies, remote signals or barrier semaphores. Data moves between devices by JAX's collectives and lax.ppermute only.
A program may use at most 192 MiB of HBM per device.

```python
import jax
import jax.numpy as jnp
from jax import lax

HD = 128
TILE = 256
HEADS = 16
TOKENS = 4096


def block_scale(own_key, dims, cuts, low, top_value):
    def one(axis_at, parts):
        draws = jax.random.uniform(jax.random.fold_in(jax.random.fold_in(own_key, 6), axis_at), (parts,), jnp.float32, low / len(cuts), top_value / len(cuts))
        return jnp.repeat(jnp.exp(draws), dims[axis_at] // parts).reshape((-1,) + (1,) * (len(dims) - axis_at - 1))

    loudness = one(*cuts[0])
    for cut in cuts[1:]:
        loudness = loudness * one(*cut)
    return loudness


def scatter_about(stream_key, extent, scale, reach, split=(), dtype=jnp.bfloat16):
    factor_of = block_scale(stream_key, extent, split, -0.22, 0.18) if split else 1.0
    entries = jax.random.normal(stream_key, extent, jnp.float32) * scale * factor_of
    return jnp.minimum(jnp.maximum(entries, -reach), reach).astype(dtype)


def setup_inputs(seed: int = 0) -> dict:
    splits = jax.random.split(jax.random.key(seed), 5)
    queries = scatter_about(splits[0], (HEADS, TOKENS, HD), ((HD * TOKENS) ** -0.16666667), 1.75, ((0, 2), (1, 16)))
    key_rows = scatter_about(splits[1], (HEADS, TOKENS, HD), ((HD * TOKENS) ** -0.16666667), 1.75, ((0, 2), (1, 16)))
    value_rows = scatter_about(splits[2], (HEADS, TOKENS, HD), ((HD * TOKENS) ** -0.16666667), 1.75, ((0, 2), (1, 16)))
    grad_out = scatter_about(splits[3], (HEADS, TOKENS, HD), ((HD * TOKENS) ** -0.16666667), 1.75, ((0, 2), (1, 16)))
    return {"queries": queries, "key_rows": key_rows, "value_rows": value_rows, "grad_out": grad_out}


def rounded(array):
    return lax.optimization_barrier(array.astype(jnp.bfloat16)).astype(jnp.float32)


def tile_grads(pieces):
    query_tile, key_tile, value_tile, grad_tile, earlier_states, later_states = pieces
    causal = jnp.arange(TILE)[:, None] >= jnp.arange(TILE)[None, :]
    out_scores = jnp.einsum("hta,hsa->hts", grad_tile, value_tile)
    out_scores = rounded(jnp.where(causal[None], out_scores, 0.0))
    attn_scores = jnp.einsum("hta,hsa->hts", query_tile, key_tile)
    attn_scores = rounded(jnp.where(causal[None], attn_scores, 0.0))
    grad_query = jnp.einsum("hts,hsa->hta", out_scores, key_tile) + jnp.einsum("htb,hab->hta", grad_tile, earlier_states)
    grad_key = jnp.einsum("hts,hta->hsa", out_scores, query_tile) + jnp.einsum("hsb,hab->hsa", value_tile, later_states)
    grad_value = jnp.einsum("hts,htb->hsb", attn_scores, grad_tile) + jnp.einsum("hsa,hab->hsb", key_tile, later_states)
    return (grad_query.astype(jnp.bfloat16), grad_key.astype(jnp.bfloat16), grad_value.astype(jnp.bfloat16))


def tiles_of(array):
    tile_count = TOKENS // TILE
    return array.astype(jnp.float32).reshape(HEADS, tile_count, TILE, HD).transpose(1, 0, 2, 3)


def reference(queries, key_rows, value_rows, grad_out):
    query_tiles = tiles_of(queries)
    key_tiles = tiles_of(key_rows)
    value_tiles = tiles_of(value_rows)
    grad_tiles = tiles_of(grad_out)
    key_state = jnp.einsum("jhsa,jhsb->jhab", key_tiles, value_tiles)
    query_state = jnp.einsum("jhta,jhtb->jhab", query_tiles, grad_tiles)
    zero_state = jnp.zeros((1, HEADS, HD, HD), jnp.float32)
    earlier_states = jnp.concatenate([zero_state, jnp.cumsum(key_state, 0)[:-1]], 0)
    later_states = jnp.concatenate([jnp.cumsum(query_state[::-1], 0)[::-1][1:], zero_state], 0)
    results = lax.map(tile_grads, (query_tiles, key_tiles, value_tiles, grad_tiles, rounded(earlier_states), rounded(later_states)))
    return tuple(result.transpose(1, 0, 2, 3).reshape(HEADS, TOKENS, HD) for result in results)
```

```python
import jax
import jax.numpy as jnp
from jax import lax
from jax.experimental import pallas as pl
from jax.experimental.pallas import tpu as pltpu
from jax.sharding import PartitionSpec as P

TILE = 256
SPEC = P("head", "seq", None)
F32 = jnp.float32
BF16 = jnp.bfloat16


def entering(x, axis, combine, identity, reverse):
    count, place = (lax.axis_size(axis), lax.axis_index(axis))
    everything = lax.all_gather(x, axis)
    start = jnp.broadcast_to(jnp.asarray(identity, x.dtype), x.shape)

    def turn(k, before):
        at = count - 1 - k if reverse else k
        reached = at > place if reverse else at < place
        new = combine(before, everything[at])
        return jnp.where(reached, new, before)

    return lax.fori_loop(0, count, turn, start)


def add_states(earlier, latter):
    return earlier + latter


def plain_body(queries, key_rows, value_rows, grad_out):
    head_count, tokens, head_width = queries.shape
    tile_count = tokens // TILE
    tile_shape = (head_count, tile_count, TILE, head_width)
    query_tiles = queries.reshape(tile_shape)
    key_tiles = key_rows.reshape(tile_shape)
    value_tiles = value_rows.reshape(tile_shape)
    grad_tiles = grad_out.reshape(tile_shape)

    def product(rule, a, b):
        return jnp.einsum(rule, a, b, preferred_element_type=F32)

    key_state = product("hjsa,hjsb->hjab", key_tiles, value_tiles)
    query_state = product("hjta,hjtb->hjab", query_tiles, grad_tiles)
    local_keys = jnp.sum(key_state, 1)
    local_queries = jnp.sum(query_state, 1)
    blank_state = jnp.zeros_like(local_keys)
    incoming = entering(local_keys, "seq", add_states, blank_state, False)
    outgoing = entering(local_queries, "seq", add_states, blank_state, True)
    zero_state = jnp.zeros((head_count, 1, head_width, head_width), F32)
    earlier_states = incoming[:, None] + jnp.concatenate(
        [zero_state, jnp.cumsum(key_state, 1)[:, :-1]], 1
    )
    later_states = outgoing[:, None] + jnp.concatenate(
        [jnp.cumsum(query_state[:, ::-1], 1)[:, ::-1][:, 1:], zero_state], 1
    )
    earlier_states = earlier_states.astype(BF16)
    later_states = later_states.astype(BF16)
    causal = (jnp.arange(TILE)[:, None] >= jnp.arange(TILE)[None, :])[None, None]
    out_scores = product("hjta,hjsa->hjts", grad_tiles, value_tiles)
    out_scores = jnp.where(causal, out_scores, 0.0).astype(BF16)
    attn_scores = product("hjta,hjsa->hjts", query_tiles, key_tiles)
    attn_scores = jnp.where(causal, attn_scores, 0.0).astype(BF16)
    grad_query = product("hjts,hjsa->hjta", out_scores, key_tiles)
    grad_query = grad_query + product("hjtb,hjab->hjta", grad_tiles, earlier_states)
    grad_key = product("hjts,hjta->hjsa", out_scores, query_tiles)
    grad_key = grad_key + product("hjsb,hjab->hjsa", value_tiles, later_states)
    grad_value = product("hjts,hjtb->hjsb", attn_scores, grad_tiles)
    grad_value = grad_value + product("hjsa,hjab->hjsb", key_tiles, later_states)
    flat_shape = (head_count, tokens, head_width)
    return tuple(
        x.astype(BF16).reshape(flat_shape) for x in (grad_query, grad_key, grad_value)
    )


def dot(a, b, da, db):
    return lax.dot_general(a, b, (((da,), (db,)), ((), ())), preferred_element_type=F32)


def state_kernel(place, q, k, v, g, out):
    out[0, 0] = dot(k[0], v[0], 0, 0)
    out[0, 1] = dot(q[0], g[0], 0, 0)


def states_of(place, q, k, v, g, slots, other):
    _, tokens, width = q.shape

    def head(i, place):
        core = 1 - place[0] if other else place[0]
        return core * slots + (i ^ place[1])

    rows = pl.BlockSpec((1, tokens, width), lambda i, place: (head(i, place), 0, 0))
    return pl.pallas_call(
        state_kernel,
        out_shape=jax.ShapeDtypeStruct((slots, 2, width, width), F32),
        grid_spec=pltpu.PrefetchScalarGridSpec(
            num_scalar_prefetch=1,
            grid=(slots,),
            in_specs=[rows] * 4,
            out_specs=pl.BlockSpec((1, 2, width, width), lambda i, place: (i, 0, 0, 0)),
        ),
        cost_estimate=pl.CostEstimate(
            flops=slots * 4 * tokens * width * width,
            bytes_accessed=slots * (8 * tokens * width + 8 * width * width),
            transcendentals=0,
        ),
    )(place, q, k, v, g)


def local_kernel(q, k, v, g, gq, gk, gv):
    tokens = q.shape[1]
    row = lax.broadcasted_iota(jnp.int32, (tokens, tokens), 0)
    col = lax.broadcasted_iota(jnp.int32, (tokens, tokens), 1)
    q, k, v, g = q[0], k[0], v[0], g[0]
    score = jnp.where(row >= col, dot(g, v, 1, 1), 0.0).astype(BF16)
    gq[0] = dot(score, k, 1, 0)
    score = jnp.where(row <= col, dot(v, g, 1, 1), 0.0).astype(BF16)
    gk[0] = dot(score, q, 1, 0)
    score = jnp.where(row <= col, dot(k, q, 1, 1), 0.0).astype(BF16)
    gv[0] = dot(score, g, 1, 0)


def local_parts(q, k, v, g):
    heads, tokens, width = q.shape
    rows = pl.BlockSpec((1, tokens, width), lambda i: (i, 0, 0))
    return pl.pallas_call(
        local_kernel,
        out_shape=[jax.ShapeDtypeStruct(q.shape, F32)] * 3,
        grid=(heads,),
        in_specs=[rows] * 4,
        out_specs=[rows] * 3,
        cost_estimate=pl.CostEstimate(
            flops=heads * 12 * tokens * tokens * width,
            bytes_accessed=heads * 20 * tokens * width,
            transcendentals=0,
        ),
    )(q, k, v, g)


def final_kernel(place, k, v, g, lq, lk, lv, own, other, gq, gk, gv):
    mine = pl.program_id(0) < pl.num_programs(0) // 2
    state = jnp.where(mine, own[0], other[0]).astype(BF16)
    earlier, later = state[0], state[1]
    gq[0] = (lq[0] + dot(g[0], earlier, 1, 1)).astype(BF16)
    gk[0] = (lk[0] + dot(v[0], later, 1, 1)).astype(BF16)
    gv[0] = (lv[0] + dot(k[0], later, 1, 0)).astype(BF16)


def final_sums(place, k, v, g, parts, own, other):
    heads, tokens, width = k.shape
    slots = own.shape[0]

    def head(i, place):
        core = place[0] ^ (i // slots)
        return core * slots + ((i % slots) ^ place[1])

    rows = pl.BlockSpec((1, tokens, width), lambda i, place: (head(i, place), 0, 0))
    first = pl.BlockSpec(
        (1, 2, width, width), lambda i, place: (jnp.minimum(i, slots - 1), 0, 0, 0)
    )
    second = pl.BlockSpec(
        (1, 2, width, width), lambda i, place: (jnp.maximum(i - slots, 0), 0, 0, 0)
    )
    return pl.pallas_call(
        final_kernel,
        out_shape=[jax.ShapeDtypeStruct(k.shape, BF16)] * 3,
        grid_spec=pltpu.PrefetchScalarGridSpec(
            num_scalar_prefetch=1,
            grid=(heads,),
            in_specs=[rows] * 6 + [first, second],
            out_specs=[rows] * 3,
        ),
        cost_estimate=pl.CostEstimate(
            flops=heads * 6 * tokens * width * width,
            bytes_accessed=heads * (24 * tokens * width + 8 * width * width),
            transcendentals=0,
        ),
    )(place, k, v, g, *parts, own, other)


def swap(x, mask):
    count = lax.axis_size("seq")
    return lax.ppermute(x, "seq", [(i, i ^ mask) for i in range(count)])


def sliced_body(group):
    def body(queries, key_rows, value_rows, grad_out):
        count, index = lax.axis_size("seq"), lax.axis_index("seq")
        slots = group
        core = index & 1
        rank = (index >> 1) & (group - 1)
        place = jnp.stack([core, rank]).astype(jnp.int32)
        data = (queries, key_rows, value_rows, grad_out)

        away = states_of(place, *data, slots, True)
        came = swap(away, 1)
        keep = states_of(place, *data, slots, False)
        total = came + keep

        held = [total[0]] + [swap(total[j], 2 * j) for j in range(1, group)]
        parts = local_parts(*data)

        block = sum(held[1:], held[0])
        keys, rests = block[0], block[1]
        carry = jnp.zeros_like(block)
        bit = 2 * group
        while bit < count:
            upper = (index & bit) != 0
            if 2 * bit < count:
                got = swap(jnp.stack([keys, rests]), bit)
                keys, rests = keys + got[0], rests + got[1]
                got_keys, got_rests = got[0], got[1]
            else:
                got_keys = got_rests = swap(jnp.where(upper, rests, keys), bit)
            carry = carry + jnp.stack(
                [jnp.where(upper, got_keys, 0.0), jnp.where(upper, 0.0, got_rests)]
            )
            bit *= 2

        def outside(j):
            earlier, later = carry[0], carry[1]
            for i in range(group):
                if i != j:
                    before = (rank ^ i) < (rank ^ j)
                    earlier = earlier + jnp.where(before, held[i][0], 0.0)
                    later = later + jnp.where(before, 0.0, held[i][1])
            return jnp.stack([earlier, later])

        around = jnp.stack(
            [outside(0)] + [swap(outside(j), 2 * j) for j in range(1, group)]
        )
        first = core == 0
        mine = around + jnp.stack(
            [jnp.where(first, 0.0, came[:, 0]), jnp.where(first, came[:, 1], 0.0)], 1
        )
        theirs = around + jnp.stack(
            [jnp.where(first, keep[:, 0], 0.0), jnp.where(first, 0.0, keep[:, 1])], 1
        )
        other = swap(theirs, 1)
        return tuple(final_sums(place, key_rows, value_rows, grad_out, parts, mine, other))

    return body


def solution(mesh):
    count = mesh.shape["seq"]

    def run(queries, key_rows, value_rows, grad_out):
        heads = queries.shape[0] // mesh.shape["head"]
        tokens = queries.shape[1] // count
        group = heads // 2
        powers = all(n > 0 and n & (n - 1) == 0 for n in (count, group))
        fits = powers and heads == 2 * group and tokens == TILE and count >= 4 * group
        body = sliced_body(group) if fits else plain_body
        return jax.shard_map(
            body, mesh=mesh, in_specs=(SPEC,) * 4, out_specs=(SPEC,) * 3, check_vma=False
        )(queries, key_rows, value_rows, grad_out)

    return run
```

```python
import functools

import jax
import jax.numpy as jnp
from jax import lax
from jax.experimental import pallas as pl
from jax.experimental.pallas import tpu as pltpu
from jax.sharding import PartitionSpec as P

TILE = 256
SPEC = P("head", "seq", None)
F32 = jnp.float32
BF16 = jnp.bfloat16


def entering(x, axis, combine, identity, reverse):
    count, place = (lax.axis_size(axis), lax.axis_index(axis))
    everything = lax.all_gather(x, axis)
    start = jnp.broadcast_to(jnp.asarray(identity, x.dtype), x.shape)

    def turn(k, before):
        at = count - 1 - k if reverse else k
        reached = at > place if reverse else at < place
        new = combine(before, everything[at])
        return jnp.where(reached, new, before)

    return lax.fori_loop(0, count, turn, start)


def add_states(earlier, latter):
    return earlier + latter


def plain_body(queries, key_rows, value_rows, grad_out):
    head_count, tokens, head_width = queries.shape
    tile_count = tokens // TILE
    tile_shape = (head_count, tile_count, TILE, head_width)
    query_tiles = queries.reshape(tile_shape)
    key_tiles = key_rows.reshape(tile_shape)
    value_tiles = value_rows.reshape(tile_shape)
    grad_tiles = grad_out.reshape(tile_shape)

    def product(rule, a, b):
        return jnp.einsum(rule, a, b, preferred_element_type=F32)

    key_state = product("hjsa,hjsb->hjab", key_tiles, value_tiles)
    query_state = product("hjta,hjtb->hjab", query_tiles, grad_tiles)
    local_keys = jnp.sum(key_state, 1)
    local_queries = jnp.sum(query_state, 1)
    blank_state = jnp.zeros_like(local_keys)
    incoming = entering(local_keys, "seq", add_states, blank_state, False)
    outgoing = entering(local_queries, "seq", add_states, blank_state, True)
    zero_state = jnp.zeros((head_count, 1, head_width, head_width), F32)
    earlier_states = incoming[:, None] + jnp.concatenate(
        [zero_state, jnp.cumsum(key_state, 1)[:, :-1]], 1
    )
    later_states = outgoing[:, None] + jnp.concatenate(
        [jnp.cumsum(query_state[:, ::-1], 1)[:, ::-1][:, 1:], zero_state], 1
    )
    earlier_states = earlier_states.astype(BF16)
    later_states = later_states.astype(BF16)
    causal = (jnp.arange(TILE)[:, None] >= jnp.arange(TILE)[None, :])[None, None]
    out_scores = product("hjta,hjsa->hjts", grad_tiles, value_tiles)
    out_scores = jnp.where(causal, out_scores, 0.0).astype(BF16)
    attn_scores = product("hjta,hjsa->hjts", query_tiles, key_tiles)
    attn_scores = jnp.where(causal, attn_scores, 0.0).astype(BF16)
    grad_query = product("hjts,hjsa->hjta", out_scores, key_tiles)
    grad_query = grad_query + product("hjtb,hjab->hjta", grad_tiles, earlier_states)
    grad_key = product("hjts,hjta->hjsa", out_scores, query_tiles)
    grad_key = grad_key + product("hjsb,hjab->hjsa", value_tiles, later_states)
    grad_value = product("hjts,hjtb->hjsb", attn_scores, grad_tiles)
    grad_value = grad_value + product("hjsa,hjab->hjsb", key_tiles, later_states)
    flat_shape = (head_count, tokens, head_width)
    return tuple(
        x.astype(BF16).reshape(flat_shape) for x in (grad_query, grad_key, grad_value)
    )


WHOLE = pl.BlockSpec(memory_space=pltpu.VMEM)
PLACED = pl.BlockSpec(memory_space=pl.ANY)
ROOM = pltpu.CompilerParams(vmem_limit_bytes=16 * 2**20)


def near(x):
    return pltpu.with_memory_space_constraint(x, pltpu.VMEM)


def dot(a, b, da, db):
    return lax.dot_general(a, b, (((da,), (db,)), ((), ())), preferred_element_type=F32)


def head_of(slots, slot, other):
    index = lax.axis_index("seq")
    core = 1 - (index & 1) if other else index & 1
    return core * slots + (((index >> 1) & (slots - 1)) ^ slot)


def state_kernel(q, k, v, g, qs, ks, vs, gs, out, sems, *, slots, other):
    copies = []
    for i in range(slots):
        head = head_of(slots, i, other)
        row = []
        for n, (far, close) in enumerate(((k, ks), (v, vs), (q, qs), (g, gs))):
            row.append(pltpu.make_async_copy(far.at[head], close.at[i], sems.at[i, n]))
            row[-1].start()
        copies.append(row)
    for i in range(slots):
        copies[i][0].wait()
        copies[i][1].wait()
        out[i, 0] = dot(ks[i], vs[i], 0, 0)
        copies[i][2].wait()
        copies[i][3].wait()
        out[i, 1] = dot(qs[i], gs[i], 0, 0)


def states_of(data, slots, other):
    _, tokens, width = data[0].shape
    rows = pltpu.VMEM((slots, tokens, width), BF16)
    return pl.pallas_call(
        functools.partial(state_kernel, slots=slots, other=other),
        out_shape=[rows] * 4 + [pltpu.VMEM((slots, 2, width, width), F32)],
        in_specs=[PLACED] * 4,
        out_specs=[WHOLE] * 5,
        scratch_shapes=[pltpu.SemaphoreType.DMA((slots, 4))],
        compiler_params=ROOM,
        cost_estimate=pl.CostEstimate(
            flops=slots * 4 * tokens * width * width,
            bytes_accessed=slots * 8 * tokens * width,
            transcendentals=0,
        ),
    )(*data)


def total_kernel(came, keep, *outs):
    for i, out in enumerate(outs):
        out[...] = came[i] + keep[i]


def totals_of(came, keep):
    slots, _, width, _ = keep.shape
    return pl.pallas_call(
        total_kernel,
        out_shape=[pltpu.VMEM((2, width, width), F32)] * slots,
        in_specs=[WHOLE] * 2,
        out_specs=[WHOLE] * slots,
        compiler_params=ROOM,
    )(near(came), near(keep))


def local_kernel(qa, ka, va, ga, qb, kb, vb, gb, after, *outs):
    slots, tokens, _ = qa.shape
    row = lax.broadcasted_iota(jnp.int32, (tokens, tokens), 0)
    col = lax.broadcasted_iota(jnp.int32, (tokens, tokens), 1)
    for half, (qs, ks, vs, gs) in enumerate(((qa, ka, va, ga), (qb, kb, vb, gb))):
        gq, gk, gv = outs[3 * half : 3 * half + 3]
        for i in range(slots):
            q, k, v, g = qs[i], ks[i], vs[i], gs[i]
            score = jnp.where(row >= col, dot(g, v, 1, 1), 0.0).astype(BF16)
            gq[i] = dot(score, k, 1, 0)
            score = jnp.where(row <= col, dot(v, g, 1, 1), 0.0).astype(BF16)
            gk[i] = dot(score, q, 1, 0)
            score = jnp.where(row <= col, dot(k, q, 1, 1), 0.0).astype(BF16)
            gv[i] = dot(score, g, 1, 0)


def local_parts(own, other, after):
    slots, tokens, width = own[0].shape
    out = pl.pallas_call(
        local_kernel,
        out_shape=[pltpu.VMEM(own[0].shape, F32)] * 6,
        in_specs=[WHOLE] * 8 + [PLACED],
        out_specs=[WHOLE] * 6,
        compiler_params=ROOM,
        cost_estimate=pl.CostEstimate(
            flops=slots * 24 * tokens * tokens * width,
            bytes_accessed=slots * 40 * tokens * width,
            transcendentals=0,
        ),
    )(*[near(x) for x in own], *[near(x) for x in other], near(after))
    return out[:3], out[3:]


def block_kernel(after, *refs):
    out = refs[-1]
    total = refs[0][...]
    for x in refs[1:-1]:
        total = total + x[...]
    out[...] = total


def block_sum(held, after):
    return pl.pallas_call(
        block_kernel,
        out_shape=pltpu.VMEM(held[0].shape, F32),
        in_specs=[PLACED] + [WHOLE] * len(held),
        out_specs=WHOLE,
        compiler_params=ROOM,
    )(near(after), *[near(x) for x in held])


def final_kernel(k, v, g, lq, lk, lv, state, *refs, other):
    gq, gk, gv, bq, bk, bv, sems = refs[-7:]
    slots = k.shape[0]
    copies = []
    for i in range(slots):
        earlier, later = state[i, 0].astype(BF16), state[i, 1].astype(BF16)
        head = head_of(slots, i, other)
        bq[i] = (lq[i] + dot(g[i], earlier, 1, 1)).astype(BF16)
        bk[i] = (lk[i] + dot(v[i], later, 1, 1)).astype(BF16)
        bv[i] = (lv[i] + dot(k[i], later, 1, 0)).astype(BF16)
        for n, (close, far) in enumerate(((bq, gq), (bk, gk), (bv, gv))):
            copies.append(pltpu.make_async_copy(close.at[i], far.at[head], sems.at[i, n]))
            copies[-1].start()
    for copy in copies:
        copy.wait()


def final_sums(rows, parts, state, heads, other, filled=()):
    _, k, v, g = rows
    slots, tokens, width = k.shape
    return pl.pallas_call(
        functools.partial(final_kernel, other=other),
        out_shape=[jax.ShapeDtypeStruct((heads, tokens, width), BF16)] * 3,
        in_specs=[WHOLE] * 7 + [PLACED] * len(filled),
        out_specs=[PLACED] * 3,
        input_output_aliases={7 + n: n for n in range(len(filled))},
        scratch_shapes=[pltpu.VMEM(k.shape, BF16)] * 3
        + [pltpu.SemaphoreType.DMA((slots, 3))],
        compiler_params=ROOM,
        cost_estimate=pl.CostEstimate(
            flops=slots * 6 * tokens * width * width,
            bytes_accessed=slots * 6 * tokens * width,
            transcendentals=0,
        ),
    )(*[near(x) for x in (k, v, g, *parts, state)], *filled)


def swap(x, mask):
    count = lax.axis_size("seq")
    return lax.ppermute(x, "seq", [(i, i ^ mask) for i in range(count)])


def sliced_body(group):
    def body(queries, key_rows, value_rows, grad_out):
        count, index = lax.axis_size("seq"), lax.axis_index("seq")
        slots = group
        core = index & 1
        rank = (index >> 1) & (group - 1)
        data = (queries, key_rows, value_rows, grad_out)

        *away_rows, away = states_of(data, slots, True)
        came = swap(away, 1)
        *keep_rows, keep = states_of(data, slots, False)
        total = totals_of(came, keep)

        held = [total[0]] + [swap(total[j], 2 * j) for j in range(1, group)]
        own_parts, other_parts = local_parts(keep_rows, away_rows, total[0])

        block = block_sum(held, own_parts[0])
        keys, rests = block[0], block[1]
        carry = jnp.zeros_like(block)
        bit = 2 * group
        while bit < count:
            upper = (index & bit) != 0
            if 2 * bit < count:
                got = swap(jnp.stack([keys, rests]), bit)
                keys, rests = keys + got[0], rests + got[1]
                got_keys, got_rests = got[0], got[1]
            else:
                got_keys = got_rests = swap(jnp.where(upper, rests, keys), bit)
            carry = carry + jnp.stack(
                [jnp.where(upper, got_keys, 0.0), jnp.where(upper, 0.0, got_rests)]
            )
            bit *= 2

        def outside(j):
            earlier, later = carry[0], carry[1]
            for i in range(group):
                if i != j:
                    before = (rank ^ i) < (rank ^ j)
                    earlier = earlier + jnp.where(before, held[i][0], 0.0)
                    later = later + jnp.where(before, 0.0, held[i][1])
            return jnp.stack([earlier, later])

        around = jnp.stack(
            [outside(0)] + [swap(outside(j), 2 * j) for j in range(1, group)]
        )
        first = core == 0
        mine = around + jnp.stack(
            [jnp.where(first, 0.0, came[:, 0]), jnp.where(first, came[:, 1], 0.0)], 1
        )
        theirs = around + jnp.stack(
            [jnp.where(first, keep[:, 0], 0.0), jnp.where(first, 0.0, keep[:, 1])], 1
        )
        other = swap(theirs, 1)
        done = final_sums(keep_rows, own_parts, mine, queries.shape[0], False)
        return tuple(
            final_sums(away_rows, other_parts, other, queries.shape[0], True, done)
        )

    return body


def solution(mesh):
    count = mesh.shape["seq"]

    def run(queries, key_rows, value_rows, grad_out):
        heads = queries.shape[0] // mesh.shape["head"]
        tokens = queries.shape[1] // count
        group = heads // 2
        powers = all(n > 0 and n & (n - 1) == 0 for n in (count, group))
        fits = powers and heads == 2 * group and tokens == TILE and count >= 4 * group
        body = sliced_body(group) if fits else plain_body
        return jax.shard_map(
            body, mesh=mesh, in_specs=(SPEC,) * 4, out_specs=(SPEC,) * 3, check_vma=False
        )(queries, key_rows, value_rows, grad_out)

    return run
```

```python
import functools

import jax
import jax.numpy as jnp
from jax import lax
from jax.experimental import pallas as pl
from jax.experimental.pallas import tpu as pltpu
from jax.sharding import PartitionSpec as P

TILE = 256
SPEC = P("head", "seq", None)
F32 = jnp.float32
BF16 = jnp.bfloat16


def entering(x, axis, combine, identity, reverse):
    count, place = (lax.axis_size(axis), lax.axis_index(axis))
    everything = lax.all_gather(x, axis)
    start = jnp.broadcast_to(jnp.asarray(identity, x.dtype), x.shape)

    def turn(k, before):
        at = count - 1 - k if reverse else k
        reached = at > place if reverse else at < place
        new = combine(before, everything[at])
        return jnp.where(reached, new, before)

    return lax.fori_loop(0, count, turn, start)


def add_states(earlier, latter):
    return earlier + latter


def plain_body(queries, key_rows, value_rows, grad_out):
    head_count, tokens, head_width = queries.shape
    tile_count = tokens // TILE
    tile_shape = (head_count, tile_count, TILE, head_width)
    query_tiles = queries.reshape(tile_shape)
    key_tiles = key_rows.reshape(tile_shape)
    value_tiles = value_rows.reshape(tile_shape)
    grad_tiles = grad_out.reshape(tile_shape)

    def product(rule, a, b):
        return jnp.einsum(rule, a, b, preferred_element_type=F32)

    key_state = product("hjsa,hjsb->hjab", key_tiles, value_tiles)
    query_state = product("hjta,hjtb->hjab", query_tiles, grad_tiles)
    local_keys = jnp.sum(key_state, 1)
    local_queries = jnp.sum(query_state, 1)
    blank_state = jnp.zeros_like(local_keys)
    incoming = entering(local_keys, "seq", add_states, blank_state, False)
    outgoing = entering(local_queries, "seq", add_states, blank_state, True)
    zero_state = jnp.zeros((head_count, 1, head_width, head_width), F32)
    earlier_states = incoming[:, None] + jnp.concatenate(
        [zero_state, jnp.cumsum(key_state, 1)[:, :-1]], 1
    )
    later_states = outgoing[:, None] + jnp.concatenate(
        [jnp.cumsum(query_state[:, ::-1], 1)[:, ::-1][:, 1:], zero_state], 1
    )
    earlier_states = earlier_states.astype(BF16)
    later_states = later_states.astype(BF16)
    causal = (jnp.arange(TILE)[:, None] >= jnp.arange(TILE)[None, :])[None, None]
    out_scores = product("hjta,hjsa->hjts", grad_tiles, value_tiles)
    out_scores = jnp.where(causal, out_scores, 0.0).astype(BF16)
    attn_scores = product("hjta,hjsa->hjts", query_tiles, key_tiles)
    attn_scores = jnp.where(causal, attn_scores, 0.0).astype(BF16)
    grad_query = product("hjts,hjsa->hjta", out_scores, key_tiles)
    grad_query = grad_query + product("hjtb,hjab->hjta", grad_tiles, earlier_states)
    grad_key = product("hjts,hjta->hjsa", out_scores, query_tiles)
    grad_key = grad_key + product("hjsb,hjab->hjsa", value_tiles, later_states)
    grad_value = product("hjts,hjtb->hjsb", attn_scores, grad_tiles)
    grad_value = grad_value + product("hjsa,hjab->hjsb", key_tiles, later_states)
    flat_shape = (head_count, tokens, head_width)
    return tuple(
        x.astype(BF16).reshape(flat_shape) for x in (grad_query, grad_key, grad_value)
    )


WHOLE = pl.BlockSpec(memory_space=pltpu.VMEM)
PLACED = pl.BlockSpec(memory_space=pl.ANY)
FAR = pl.BlockSpec(memory_space=pltpu.HBM)
ROOM = pltpu.CompilerParams(vmem_limit_bytes=16 * 2**20)


def near(x):
    return pltpu.with_memory_space_constraint(x, pltpu.VMEM)


def far(x):
    return pltpu.with_memory_space_constraint(x, pltpu.HBM)


def dot(a, b, da, db):
    return lax.dot_general(a, b, (((da,), (db,)), ((), ())), preferred_element_type=F32)


def head_of(slots, slot, other):
    index = lax.axis_index("seq")
    core = 1 - (index & 1) if other else index & 1
    return core * slots + (((index >> 1) & (slots - 1)) ^ slot)


def state_kernel(q, k, v, g, qs, ks, vs, gs, out, sems, *, slots, other):
    copies = []
    for i in range(slots):
        head = head_of(slots, i, other)
        row = []
        for n, (there, here) in enumerate(((k, ks), (v, vs), (q, qs), (g, gs))):
            row.append(pltpu.make_async_copy(there.at[head], here.at[i], sems.at[i, n]))
            row[-1].start()
        copies.append(row)
    for i in range(slots):
        copies[i][0].wait()
        copies[i][1].wait()
        out[i, 0] = dot(ks[i], vs[i], 0, 0)
        copies[i][2].wait()
        copies[i][3].wait()
        out[i, 1] = dot(qs[i], gs[i], 0, 0)


def states_of(data, slots, other):
    _, tokens, width = data[0].shape
    rows = pltpu.VMEM((slots, tokens, width), BF16)
    return pl.pallas_call(
        functools.partial(state_kernel, slots=slots, other=other),
        out_shape=[rows] * 4 + [pltpu.VMEM((slots, 2, width, width), F32)],
        in_specs=[FAR] * 4,
        out_specs=[WHOLE] * 5,
        scratch_shapes=[pltpu.SemaphoreType.DMA((slots, 4))],
        compiler_params=ROOM,
        cost_estimate=pl.CostEstimate(
            flops=slots * 4 * tokens * width * width,
            bytes_accessed=slots * 8 * tokens * width,
            transcendentals=0,
        ),
    )(*[far(x) for x in data])


def total_kernel(came, keep, *outs):
    for i, out in enumerate(outs):
        out[...] = came[i] + keep[i]


def totals_of(came, keep):
    slots, _, width, _ = keep.shape
    return pl.pallas_call(
        total_kernel,
        out_shape=[pltpu.VMEM((2, width, width), F32)] * slots,
        in_specs=[WHOLE] * 2,
        out_specs=[WHOLE] * slots,
        compiler_params=ROOM,
    )(near(came), near(keep))


def local_kernel(qa, ka, va, ga, qb, kb, vb, gb, after, *outs):
    slots, tokens, _ = qa.shape
    row = lax.broadcasted_iota(jnp.int32, (tokens, tokens), 0)
    col = lax.broadcasted_iota(jnp.int32, (tokens, tokens), 1)
    for half, (qs, ks, vs, gs) in enumerate(((qa, ka, va, ga), (qb, kb, vb, gb))):
        gq, gk, gv = outs[3 * half : 3 * half + 3]
        for i in range(slots):
            q, k, v, g = qs[i], ks[i], vs[i], gs[i]
            score = jnp.where(row >= col, dot(g, v, 1, 1), 0.0).astype(BF16)
            gq[i] = dot(score, k, 1, 0)
            score = jnp.where(row <= col, dot(v, g, 1, 1), 0.0).astype(BF16)
            gk[i] = dot(score, q, 1, 0)
            score = jnp.where(row <= col, dot(k, q, 1, 1), 0.0).astype(BF16)
            gv[i] = dot(score, g, 1, 0)


def local_parts(own, other, after):
    slots, tokens, width = own[0].shape
    out = pl.pallas_call(
        local_kernel,
        out_shape=[pltpu.VMEM(own[0].shape, F32)] * 6,
        in_specs=[WHOLE] * 8 + [PLACED],
        out_specs=[WHOLE] * 6,
        compiler_params=ROOM,
        cost_estimate=pl.CostEstimate(
            flops=slots * 24 * tokens * tokens * width,
            bytes_accessed=slots * 40 * tokens * width,
            transcendentals=0,
        ),
    )(*[near(x) for x in own], *[near(x) for x in other], near(after))
    return out[:3], out[3:]


def block_kernel(after, *refs):
    out = refs[-1]
    total = refs[0][...]
    for x in refs[1:-1]:
        total = total + x[...]
    out[...] = total


def block_sum(held, after):
    return pl.pallas_call(
        block_kernel,
        out_shape=pltpu.VMEM(held[0].shape, F32),
        in_specs=[PLACED] + [WHOLE] * len(held),
        out_specs=WHOLE,
        compiler_params=ROOM,
    )(near(after), *[near(x) for x in held])


def final_kernel(k, v, g, lq, lk, lv, state, *refs, other):
    gq, gk, gv, bq, bk, bv, sems = refs[-7:]
    slots = k.shape[0]
    copies = []
    for i in range(slots):
        earlier, later = state[i, 0].astype(BF16), state[i, 1].astype(BF16)
        head = head_of(slots, i, other)
        bq[i] = (lq[i] + dot(g[i], earlier, 1, 1)).astype(BF16)
        bk[i] = (lk[i] + dot(v[i], later, 1, 1)).astype(BF16)
        bv[i] = (lv[i] + dot(k[i], later, 1, 0)).astype(BF16)
        for n, (here, there) in enumerate(((bq, gq), (bk, gk), (bv, gv))):
            copies.append(pltpu.make_async_copy(here.at[i], there.at[head], sems.at[i, n]))
            copies[-1].start()
    for copy in copies:
        copy.wait()


def final_sums(rows, parts, state, heads, other, filled=()):
    _, k, v, g = rows
    slots, tokens, width = k.shape
    return pl.pallas_call(
        functools.partial(final_kernel, other=other),
        out_shape=[jax.ShapeDtypeStruct((heads, tokens, width), BF16)] * 3,
        in_specs=[WHOLE] * 7 + [PLACED] * len(filled),
        out_specs=[PLACED] * 3,
        input_output_aliases={7 + n: n for n in range(len(filled))},
        scratch_shapes=[pltpu.VMEM(k.shape, BF16)] * 3
        + [pltpu.SemaphoreType.DMA((slots, 3))],
        compiler_params=ROOM,
        cost_estimate=pl.CostEstimate(
            flops=slots * 6 * tokens * width * width,
            bytes_accessed=slots * 6 * tokens * width,
            transcendentals=0,
        ),
    )(*[near(x) for x in (k, v, g, *parts, state)], *filled)


def swap(x, mask):
    count = lax.axis_size("seq")
    return lax.ppermute(x, "seq", [(i, i ^ mask) for i in range(count)])


def sliced_body(group):
    def body(queries, key_rows, value_rows, grad_out):
        count, index = lax.axis_size("seq"), lax.axis_index("seq")
        slots = group
        core = index & 1
        rank = (index >> 1) & (group - 1)
        data = (queries, key_rows, value_rows, grad_out)

        *away_rows, away = states_of(data, slots, True)
        came = swap(away, 1)
        *keep_rows, keep = states_of(data, slots, False)
        total = totals_of(came, keep)

        held = [total[0]] + [swap(total[j], 2 * j) for j in range(1, group)]
        own_parts, other_parts = local_parts(keep_rows, away_rows, total[0])

        block = block_sum(held, own_parts[0])
        keys, rests = block[0], block[1]
        carry = jnp.zeros_like(block)
        bit = 2 * group
        while bit < count:
            upper = (index & bit) != 0
            if 2 * bit < count:
                got = swap(jnp.stack([keys, rests]), bit)
                keys, rests = keys + got[0], rests + got[1]
                got_keys, got_rests = got[0], got[1]
            else:
                got_keys = got_rests = swap(jnp.where(upper, rests, keys), bit)
            carry = carry + jnp.stack(
                [jnp.where(upper, got_keys, 0.0), jnp.where(upper, 0.0, got_rests)]
            )
            bit *= 2

        def outside(j):
            earlier, later = carry[0], carry[1]
            for i in range(group):
                if i != j:
                    before = (rank ^ i) < (rank ^ j)
                    earlier = earlier + jnp.where(before, held[i][0], 0.0)
                    later = later + jnp.where(before, 0.0, held[i][1])
            return jnp.stack([earlier, later])

        around = jnp.stack(
            [outside(0)] + [swap(outside(j), 2 * j) for j in range(1, group)]
        )
        first = core == 0
        mine = around + jnp.stack(
            [jnp.where(first, 0.0, came[:, 0]), jnp.where(first, came[:, 1], 0.0)], 1
        )
        theirs = around + jnp.stack(
            [jnp.where(first, keep[:, 0], 0.0), jnp.where(first, 0.0, keep[:, 1])], 1
        )
        other = swap(theirs, 1)
        done = final_sums(keep_rows, own_parts, mine, queries.shape[0], False)
        return tuple(
            final_sums(away_rows, other_parts, other, queries.shape[0], True, done)
        )

    return body


def solution(mesh):
    count = mesh.shape["seq"]

    def run(queries, key_rows, value_rows, grad_out):
        heads = queries.shape[0] // mesh.shape["head"]
        tokens = queries.shape[1] // count
        group = heads // 2
        powers = all(n > 0 and n & (n - 1) == 0 for n in (count, group))
        fits = powers and heads == 2 * group and tokens == TILE and count >= 4 * group
        body = sliced_body(group) if fits else plain_body
        return jax.shard_map(
            body, mesh=mesh, in_specs=(SPEC,) * 4, out_specs=(SPEC,) * 3, check_vma=False
        )(queries, key_rows, value_rows, grad_out)

    return run
```

```python
import functools

import jax
import jax.numpy as jnp
from jax import lax
from jax.experimental import pallas as pl
from jax.experimental.pallas import tpu as pltpu
from jax.sharding import PartitionSpec as P

TILE = 256
SPEC = P("head", "seq", None)
F32 = jnp.float32
BF16 = jnp.bfloat16


def entering(x, axis, combine, identity, reverse):
    count, place = (lax.axis_size(axis), lax.axis_index(axis))
    everything = lax.all_gather(x, axis)
    start = jnp.broadcast_to(jnp.asarray(identity, x.dtype), x.shape)

    def turn(k, before):
        at = count - 1 - k if reverse else k
        reached = at > place if reverse else at < place
        new = combine(before, everything[at])
        return jnp.where(reached, new, before)

    return lax.fori_loop(0, count, turn, start)


def add_states(earlier, latter):
    return earlier + latter


def plain_body(queries, key_rows, value_rows, grad_out):
    head_count, tokens, head_width = queries.shape
    tile_count = tokens // TILE
    tile_shape = (head_count, tile_count, TILE, head_width)
    query_tiles = queries.reshape(tile_shape)
    key_tiles = key_rows.reshape(tile_shape)
    value_tiles = value_rows.reshape(tile_shape)
    grad_tiles = grad_out.reshape(tile_shape)

    def product(rule, a, b):
        return jnp.einsum(rule, a, b, preferred_element_type=F32)

    key_state = product("hjsa,hjsb->hjab", key_tiles, value_tiles)
    query_state = product("hjta,hjtb->hjab", query_tiles, grad_tiles)
    local_keys = jnp.sum(key_state, 1)
    local_queries = jnp.sum(query_state, 1)
    blank_state = jnp.zeros_like(local_keys)
    incoming = entering(local_keys, "seq", add_states, blank_state, False)
    outgoing = entering(local_queries, "seq", add_states, blank_state, True)
    zero_state = jnp.zeros((head_count, 1, head_width, head_width), F32)
    earlier_states = incoming[:, None] + jnp.concatenate(
        [zero_state, jnp.cumsum(key_state, 1)[:, :-1]], 1
    )
    later_states = outgoing[:, None] + jnp.concatenate(
        [jnp.cumsum(query_state[:, ::-1], 1)[:, ::-1][:, 1:], zero_state], 1
    )
    earlier_states = earlier_states.astype(BF16)
    later_states = later_states.astype(BF16)
    causal = (jnp.arange(TILE)[:, None] >= jnp.arange(TILE)[None, :])[None, None]
    out_scores = product("hjta,hjsa->hjts", grad_tiles, value_tiles)
    out_scores = jnp.where(causal, out_scores, 0.0).astype(BF16)
    attn_scores = product("hjta,hjsa->hjts", query_tiles, key_tiles)
    attn_scores = jnp.where(causal, attn_scores, 0.0).astype(BF16)
    grad_query = product("hjts,hjsa->hjta", out_scores, key_tiles)
    grad_query = grad_query + product("hjtb,hjab->hjta", grad_tiles, earlier_states)
    grad_key = product("hjts,hjta->hjsa", out_scores, query_tiles)
    grad_key = grad_key + product("hjsb,hjab->hjsa", value_tiles, later_states)
    grad_value = product("hjts,hjtb->hjsb", attn_scores, grad_tiles)
    grad_value = grad_value + product("hjsa,hjab->hjsb", key_tiles, later_states)
    flat_shape = (head_count, tokens, head_width)
    return tuple(
        x.astype(BF16).reshape(flat_shape) for x in (grad_query, grad_key, grad_value)
    )


WHOLE = pl.BlockSpec(memory_space=pltpu.VMEM)
PLACED = pl.BlockSpec(memory_space=pl.ANY)
FAR = pl.BlockSpec(memory_space=pltpu.HBM)
ROOM = pltpu.CompilerParams(vmem_limit_bytes=16 * 2**20)


def near(x):
    return pltpu.with_memory_space_constraint(x, pltpu.VMEM)


def far(x):
    return pltpu.with_memory_space_constraint(x, pltpu.HBM)


def dot(a, b, da, db):
    return lax.dot_general(a, b, (((da,), (db,)), ((), ())), preferred_element_type=F32)


def place_of(slots):
    index = lax.axis_index("seq")
    return index & 1, (index >> 1) & (slots - 1)


def away_kernel(q, k, v, g, out, qs, ks, vs, gs, sems):
    slots = out.shape[0]
    core, rank = place_of(slots)
    first = (1 - core) * slots
    copies = []
    for n, (there, here) in enumerate(((k, ks), (v, vs), (q, qs), (g, gs))):
        copies.append(pltpu.make_async_copy(there.at[pl.ds(first, slots)], here, sems.at[n]))
        copies[-1].start()
    copies[0].wait()
    copies[1].wait()
    for i in range(slots):
        out[i, 0] = dot(ks[rank ^ i], vs[rank ^ i], 0, 0)
    copies[2].wait()
    copies[3].wait()
    for i in range(slots):
        out[i, 1] = dot(qs[rank ^ i], gs[rank ^ i], 0, 0)


def keep_kernel(q, k, v, g, out):
    slots = out.shape[0]
    core, rank = place_of(slots)
    for i in range(slots):
        head = core * slots + (rank ^ i)
        out[i, 0] = dot(k[head], v[head], 0, 0)
        out[i, 1] = dot(q[head], g[head], 0, 0)


def state_call(kernel, data, slots, place, spec, scratch):
    _, tokens, width = data[0].shape
    return pl.pallas_call(
        kernel,
        out_shape=pltpu.VMEM((slots, 2, width, width), F32),
        in_specs=[spec] * 4,
        out_specs=WHOLE,
        scratch_shapes=scratch,
        compiler_params=ROOM,
        cost_estimate=pl.CostEstimate(
            flops=slots * 4 * tokens * width * width,
            bytes_accessed=slots * 8 * tokens * width,
            transcendentals=0,
        ),
    )(*[place(x) for x in data])


def away_states(data, slots):
    _, tokens, width = data[0].shape
    scratch = [pltpu.VMEM((slots, tokens, width), BF16)] * 4 + [pltpu.SemaphoreType.DMA((4,))]
    return state_call(away_kernel, data, slots, far, FAR, scratch)


def keep_states(data, slots):
    return state_call(keep_kernel, data, slots, near, WHOLE, [])


def total_kernel(came, keep, *outs):
    for i, out in enumerate(outs):
        out[...] = came[i] + keep[i]


def totals_of(came, keep):
    slots, _, width, _ = keep.shape
    return pl.pallas_call(
        total_kernel,
        out_shape=[pltpu.VMEM((2, width, width), F32)] * slots,
        in_specs=[WHOLE] * 2,
        out_specs=[WHOLE] * slots,
        compiler_params=ROOM,
    )(near(came), near(keep))


def local_kernel(qs, ks, vs, gs, after, gq, gk, gv):
    heads, tokens, _ = qs.shape
    row = lax.broadcasted_iota(jnp.int32, (tokens, tokens), 0)
    col = lax.broadcasted_iota(jnp.int32, (tokens, tokens), 1)
    for i in range(heads):
        q, k, v, g = qs[i], ks[i], vs[i], gs[i]
        score = jnp.where(row >= col, dot(g, v, 1, 1), 0.0).astype(BF16)
        gq[i] = dot(score, k, 1, 0)
        score = jnp.where(row <= col, dot(v, g, 1, 1), 0.0).astype(BF16)
        gk[i] = dot(score, q, 1, 0)
        score = jnp.where(row <= col, dot(k, q, 1, 1), 0.0).astype(BF16)
        gv[i] = dot(score, g, 1, 0)


def local_parts(data, after):
    heads, tokens, width = data[0].shape
    return pl.pallas_call(
        local_kernel,
        out_shape=[pltpu.VMEM(data[0].shape, F32)] * 3,
        in_specs=[WHOLE] * 4 + [PLACED],
        out_specs=[WHOLE] * 3,
        compiler_params=ROOM,
        cost_estimate=pl.CostEstimate(
            flops=heads * 12 * tokens * tokens * width,
            bytes_accessed=heads * 20 * tokens * width,
            transcendentals=0,
        ),
    )(*[near(x) for x in data], near(after))


def block_kernel(after, *refs):
    out = refs[-1]
    total = refs[0][...]
    for x in refs[1:-1]:
        total = total + x[...]
    out[...] = total


def block_sum(held, after):
    return pl.pallas_call(
        block_kernel,
        out_shape=pltpu.VMEM(held[0].shape, F32),
        in_specs=[PLACED] + [WHOLE] * len(held),
        out_specs=WHOLE,
        compiler_params=ROOM,
    )(near(after), *[near(x) for x in held])


def final_kernel(k, v, g, lq, lk, lv, state, *refs, other):
    gq, gk, gv, bq, bk, bv, sems = refs[-7:]
    slots = state.shape[0]
    core, rank = place_of(slots)
    first = (1 - core if other else core) * slots
    copies = []
    for i in range(slots):
        earlier, later = state[i, 0].astype(BF16), state[i, 1].astype(BF16)
        head = first + (rank ^ i)
        bq[i] = (lq[head] + dot(g[head], earlier, 1, 1)).astype(BF16)
        bk[i] = (lk[head] + dot(v[head], later, 1, 1)).astype(BF16)
        bv[i] = (lv[head] + dot(k[head], later, 1, 0)).astype(BF16)
        for n, (here, there) in enumerate(((bq, gq), (bk, gk), (bv, gv))):
            copies.append(pltpu.make_async_copy(here.at[i], there.at[head], sems.at[i, n]))
            copies[-1].start()
    for copy in copies:
        copy.wait()


def final_sums(data, parts, state, other, filled=()):
    _, tokens, width = data[0].shape
    slots = state.shape[0]
    return pl.pallas_call(
        functools.partial(final_kernel, other=other),
        out_shape=[jax.ShapeDtypeStruct(data[0].shape, BF16)] * 3,
        in_specs=[WHOLE] * 7 + [PLACED] * len(filled),
        out_specs=[PLACED] * 3,
        input_output_aliases={7 + n: n for n in range(len(filled))},
        scratch_shapes=[pltpu.VMEM((slots, tokens, width), BF16)] * 3
        + [pltpu.SemaphoreType.DMA((slots, 3))],
        compiler_params=ROOM,
        cost_estimate=pl.CostEstimate(
            flops=slots * 6 * tokens * width * width,
            bytes_accessed=slots * 6 * tokens * width,
            transcendentals=0,
        ),
    )(*[near(x) for x in (*data[1:], *parts, state)], *filled)


def swap(x, mask):
    count = lax.axis_size("seq")
    return lax.ppermute(x, "seq", [(i, i ^ mask) for i in range(count)])


def sliced_body(group):
    def body(queries, key_rows, value_rows, grad_out):
        count, index = lax.axis_size("seq"), lax.axis_index("seq")
        slots = group
        core = index & 1
        rank = (index >> 1) & (group - 1)
        data = (queries, key_rows, value_rows, grad_out)

        came = swap(away_states(data, slots), 1)
        keep = keep_states(data, slots)
        total = totals_of(came, keep)

        held = [total[0]] + [swap(total[j], 2 * j) for j in range(1, group)]
        parts = local_parts(data, total[0])

        block = block_sum(held, parts[0])
        keys, rests = block[0], block[1]
        carry = jnp.zeros_like(block)
        bit = 2 * group
        while bit < count:
            upper = (index & bit) != 0
            if 2 * bit < count:
                got = swap(jnp.stack([keys, rests]), bit)
                keys, rests = keys + got[0], rests + got[1]
                got_keys, got_rests = got[0], got[1]
            else:
                got_keys = got_rests = swap(jnp.where(upper, rests, keys), bit)
            carry = carry + jnp.stack(
                [jnp.where(upper, got_keys, 0.0), jnp.where(upper, 0.0, got_rests)]
            )
            bit *= 2

        def outside(j):
            earlier, later = carry[0], carry[1]
            for i in range(group):
                if i != j:
                    before = (rank ^ i) < (rank ^ j)
                    earlier = earlier + jnp.where(before, held[i][0], 0.0)
                    later = later + jnp.where(before, 0.0, held[i][1])
            return jnp.stack([earlier, later])

        around = jnp.stack(
            [outside(0)] + [swap(outside(j), 2 * j) for j in range(1, group)]
        )
        first = core == 0
        mine = around + jnp.stack(
            [jnp.where(first, 0.0, came[:, 0]), jnp.where(first, came[:, 1], 0.0)], 1
        )
        theirs = around + jnp.stack(
            [jnp.where(first, keep[:, 0], 0.0), jnp.where(first, 0.0, keep[:, 1])], 1
        )
        other = swap(theirs, 1)
        done = final_sums(data, parts, mine, False)
        return tuple(final_sums(data, parts, other, True, done))

    return body


def solution(mesh):
    count = mesh.shape["seq"]

    def run(queries, key_rows, value_rows, grad_out):
        heads = queries.shape[0] // mesh.shape["head"]
        tokens = queries.shape[1] // count
        group = heads // 2
        powers = all(n > 0 and n & (n - 1) == 0 for n in (count, group))
        fits = powers and heads == 2 * group and tokens == TILE and count >= 4 * group
        body = sliced_body(group) if fits else plain_body
        return jax.shard_map(
            body, mesh=mesh, in_specs=(SPEC,) * 4, out_specs=(SPEC,) * 3, check_vma=False
        )(queries, key_rows, value_rows, grad_out)

    return run
```

```python
import functools

import jax
import jax.numpy as jnp
from jax import lax
from jax.experimental import pallas as pl
from jax.experimental.pallas import tpu as pltpu
from jax.sharding import PartitionSpec as P

TILE = 256
SPEC = P("head", "seq", None)
F32 = jnp.float32
BF16 = jnp.bfloat16


def entering(x, axis, combine, identity, reverse):
    count, place = (lax.axis_size(axis), lax.axis_index(axis))
    everything = lax.all_gather(x, axis)
    start = jnp.broadcast_to(jnp.asarray(identity, x.dtype), x.shape)

    def turn(k, before):
        at = count - 1 - k if reverse else k
        reached = at > place if reverse else at < place
        new = combine(before, everything[at])
        return jnp.where(reached, new, before)

    return lax.fori_loop(0, count, turn, start)


def add_states(earlier, latter):
    return earlier + latter


def plain_body(queries, key_rows, value_rows, grad_out):
    head_count, tokens, head_width = queries.shape
    tile_count = tokens // TILE
    tile_shape = (head_count, tile_count, TILE, head_width)
    query_tiles = queries.reshape(tile_shape)
    key_tiles = key_rows.reshape(tile_shape)
    value_tiles = value_rows.reshape(tile_shape)
    grad_tiles = grad_out.reshape(tile_shape)

    def product(rule, a, b):
        return jnp.einsum(rule, a, b, preferred_element_type=F32)

    key_state = product("hjsa,hjsb->hjab", key_tiles, value_tiles)
    query_state = product("hjta,hjtb->hjab", query_tiles, grad_tiles)
    local_keys = jnp.sum(key_state, 1)
    local_queries = jnp.sum(query_state, 1)
    blank_state = jnp.zeros_like(local_keys)
    incoming = entering(local_keys, "seq", add_states, blank_state, False)
    outgoing = entering(local_queries, "seq", add_states, blank_state, True)
    zero_state = jnp.zeros((head_count, 1, head_width, head_width), F32)
    earlier_states = incoming[:, None] + jnp.concatenate(
        [zero_state, jnp.cumsum(key_state, 1)[:, :-1]], 1
    )
    later_states = outgoing[:, None] + jnp.concatenate(
        [jnp.cumsum(query_state[:, ::-1], 1)[:, ::-1][:, 1:], zero_state], 1
    )
    earlier_states = earlier_states.astype(BF16)
    later_states = later_states.astype(BF16)
    causal = (jnp.arange(TILE)[:, None] >= jnp.arange(TILE)[None, :])[None, None]
    out_scores = product("hjta,hjsa->hjts", grad_tiles, value_tiles)
    out_scores = jnp.where(causal, out_scores, 0.0).astype(BF16)
    attn_scores = product("hjta,hjsa->hjts", query_tiles, key_tiles)
    attn_scores = jnp.where(causal, attn_scores, 0.0).astype(BF16)
    grad_query = product("hjts,hjsa->hjta", out_scores, key_tiles)
    grad_query = grad_query + product("hjtb,hjab->hjta", grad_tiles, earlier_states)
    grad_key = product("hjts,hjta->hjsa", out_scores, query_tiles)
    grad_key = grad_key + product("hjsb,hjab->hjsa", value_tiles, later_states)
    grad_value = product("hjts,hjtb->hjsb", attn_scores, grad_tiles)
    grad_value = grad_value + product("hjsa,hjab->hjsb", key_tiles, later_states)
    flat_shape = (head_count, tokens, head_width)
    return tuple(
        x.astype(BF16).reshape(flat_shape) for x in (grad_query, grad_key, grad_value)
    )


WHOLE = pl.BlockSpec(memory_space=pltpu.VMEM)
PLACED = pl.BlockSpec(memory_space=pl.ANY)
FAR = pl.BlockSpec(memory_space=pltpu.HBM)
ROOM = pltpu.CompilerParams(vmem_limit_bytes=16 * 2**20)


def near(x):
    return pltpu.with_memory_space_constraint(x, pltpu.VMEM)


def far(x):
    return pltpu.with_memory_space_constraint(x, pltpu.HBM)


def dot(a, b, da, db):
    return lax.dot_general(a, b, (((da,), (db,)), ((), ())), preferred_element_type=F32)


def place_of(slots):
    index = lax.axis_index("seq")
    return index & 1, (index >> 1) & (slots - 1)


def away_kernel(q, k, v, g, out, qs, ks, vs, gs, sems):
    slots = out.shape[0]
    core, rank = place_of(slots)
    first = (1 - core) * slots
    copies = []
    for n, (there, here) in enumerate(((k, ks), (v, vs), (q, qs), (g, gs))):
        copies.append(pltpu.make_async_copy(there.at[pl.ds(first, slots)], here, sems.at[n]))
        copies[-1].start()
    copies[0].wait()
    copies[1].wait()
    for i in range(slots):
        out[i, 0] = dot(ks[rank ^ i], vs[rank ^ i], 0, 0)
    copies[2].wait()
    copies[3].wait()
    for i in range(slots):
        out[i, 1] = dot(qs[rank ^ i], gs[rank ^ i], 0, 0)


def keep_kernel(q, k, v, g, out):
    slots = out.shape[0]
    core, rank = place_of(slots)
    for i in range(slots):
        head = core * slots + (rank ^ i)
        out[i, 0] = dot(k[head], v[head], 0, 0)
        out[i, 1] = dot(q[head], g[head], 0, 0)


def state_call(kernel, data, slots, place, spec, scratch):
    _, tokens, width = data[0].shape
    return pl.pallas_call(
        kernel,
        out_shape=pltpu.VMEM((slots, 2, width, width), F32),
        in_specs=[spec] * 4,
        out_specs=WHOLE,
        scratch_shapes=scratch,
        compiler_params=ROOM,
        cost_estimate=pl.CostEstimate(
            flops=slots * 4 * tokens * width * width,
            bytes_accessed=slots * 8 * tokens * width,
            transcendentals=0,
        ),
    )(*[place(x) for x in data])


def away_states(data, slots):
    _, tokens, width = data[0].shape
    scratch = [pltpu.VMEM((slots, tokens, width), BF16)] * 4 + [pltpu.SemaphoreType.DMA((4,))]
    return state_call(away_kernel, data, slots, far, FAR, scratch)


def keep_states(data, slots):
    return state_call(keep_kernel, data, slots, near, WHOLE, [])


def total_kernel(came, keep, *refs):
    *totals, inner, outer = refs
    core, _ = place_of(len(totals))
    for i, out in enumerate(totals):
        out[...] = came[i] + keep[i]
        inner[i] = jnp.where(core == 0, came[i, 1], came[i, 0])
        outer[i] = jnp.where(core == 0, keep[i, 0], keep[i, 1])


def totals_of(came, keep):
    slots, _, width, _ = keep.shape
    return pl.pallas_call(
        total_kernel,
        out_shape=[pltpu.VMEM((2, width, width), F32)] * slots
        + [pltpu.VMEM((slots, width, width), F32)] * 2,
        in_specs=[WHOLE] * 2,
        out_specs=[WHOLE] * (slots + 2),
        compiler_params=ROOM,
    )(near(came), near(keep))


def outside_kernel(carry, *refs, slot, group):
    out = refs[-1]
    _, rank = place_of(group)
    earlier, later = carry[0], carry[1]
    for i in range(group):
        if i != slot:
            before = (rank ^ i) < (rank ^ slot)
            earlier = earlier + jnp.where(before, refs[i][0], 0.0)
            later = later + jnp.where(before, 0.0, refs[i][1])
    out[0] = earlier
    out[1] = later


def outside_of(carry, held, slot):
    return pl.pallas_call(
        functools.partial(outside_kernel, slot=slot, group=len(held)),
        out_shape=pltpu.VMEM(carry.shape, F32),
        in_specs=[WHOLE] * (1 + len(held)),
        out_specs=WHOLE,
        compiler_params=ROOM,
    )(near(carry), *[near(x) for x in held])


def share_kernel(inner, outer, *refs, slots):
    around, (mine, theirs) = refs[: len(slots)], refs[-2:]
    core, _ = place_of(inner.shape[0])
    first = core == 0
    for n, i in enumerate(slots):
        earlier, later = around[n][0], around[n][1]
        mine[n, 0] = earlier + jnp.where(first, 0.0, inner[i])
        mine[n, 1] = later + jnp.where(first, inner[i], 0.0)
        theirs[n, 0] = earlier + jnp.where(first, outer[i], 0.0)
        theirs[n, 1] = later + jnp.where(first, 0.0, outer[i])


def shares_of(inner, outer, around, slots, after=()):
    _, width, _ = inner.shape
    return pl.pallas_call(
        functools.partial(share_kernel, slots=slots),
        out_shape=[pltpu.VMEM((len(slots), 2, width, width), F32)] * 2,
        in_specs=[WHOLE] * (2 + len(slots)) + [PLACED] * len(after),
        out_specs=[WHOLE] * 2,
        compiler_params=ROOM,
    )(near(inner), near(outer), *[near(around[i]) for i in slots], *[near(x) for x in after])


def local_kernel(qs, ks, vs, gs, after, gq, gk, gv):
    heads, tokens, _ = qs.shape
    row = lax.broadcasted_iota(jnp.int32, (tokens, tokens), 0)
    col = lax.broadcasted_iota(jnp.int32, (tokens, tokens), 1)
    for i in range(heads):
        q, k, v, g = qs[i], ks[i], vs[i], gs[i]
        score = jnp.where(row >= col, dot(g, v, 1, 1), 0.0).astype(BF16)
        gq[i] = dot(score, k, 1, 0)
        score = jnp.where(row <= col, dot(v, g, 1, 1), 0.0).astype(BF16)
        gk[i] = dot(score, q, 1, 0)
        score = jnp.where(row <= col, dot(k, q, 1, 1), 0.0).astype(BF16)
        gv[i] = dot(score, g, 1, 0)


def local_parts(data, after):
    heads, tokens, width = data[0].shape
    return pl.pallas_call(
        local_kernel,
        out_shape=[pltpu.VMEM(data[0].shape, F32)] * 3,
        in_specs=[WHOLE] * 4 + [PLACED],
        out_specs=[WHOLE] * 3,
        compiler_params=ROOM,
        cost_estimate=pl.CostEstimate(
            flops=heads * 12 * tokens * tokens * width,
            bytes_accessed=heads * 20 * tokens * width,
            transcendentals=0,
        ),
    )(*[near(x) for x in data], near(after))


def block_kernel(after, *refs):
    out = refs[-1]
    total = refs[0][...]
    for x in refs[1:-1]:
        total = total + x[...]
    out[...] = total


def block_sum(held, after):
    return pl.pallas_call(
        block_kernel,
        out_shape=pltpu.VMEM(held[0].shape, F32),
        in_specs=[PLACED] + [WHOLE] * len(held),
        out_specs=WHOLE,
        compiler_params=ROOM,
    )(near(after), *[near(x) for x in held])


def final_kernel(k, v, g, lq, lk, lv, *refs, pieces, given):
    bq, bk, bv, sems = refs[-4:]
    gq, gk, gv, *marks = refs[len(pieces) + given : -4]
    for mark in marks:
        mark[...] = jnp.zeros_like(mark)
    half = k.shape[0] // 2
    core, rank = place_of(half)
    copies = []
    for state, (other, slots) in zip(refs, pieces):
        first = (1 - core if other else core) * half
        for i, slot in enumerate(slots):
            earlier, later = state[i, 0].astype(BF16), state[i, 1].astype(BF16)
            head, n = first + (rank ^ slot), len(copies) // 3
            bq[n] = (lq[head] + dot(g[head], earlier, 1, 1)).astype(BF16)
            bk[n] = (lk[head] + dot(v[head], later, 1, 1)).astype(BF16)
            bv[n] = (lv[head] + dot(k[head], later, 1, 0)).astype(BF16)
            for m, (here, there) in enumerate(((bq, gq), (bk, gk), (bv, gv))):
                copies.append(pltpu.make_async_copy(here.at[n], there.at[head], sems.at[n, m]))
                copies[-1].start()
    for copy in copies:
        copy.wait()


def final_sums(data, parts, states, pieces, filled=()):
    _, tokens, width = data[0].shape
    count = sum(len(slots) for _, slots in pieces)
    held = 6 + len(states)
    return pl.pallas_call(
        functools.partial(final_kernel, pieces=pieces, given=len(filled)),
        out_shape=[jax.ShapeDtypeStruct(data[0].shape, BF16)] * 3
        + [pltpu.VMEM((8, width), F32)] * (not filled),
        in_specs=[WHOLE] * held + [PLACED] * len(filled),
        out_specs=[PLACED] * 3 + [WHOLE] * (not filled),
        input_output_aliases={held + n: n for n in range(len(filled))},
        scratch_shapes=[pltpu.VMEM((count, tokens, width), BF16)] * 3
        + [pltpu.SemaphoreType.DMA((count, 3))],
        compiler_params=ROOM,
        cost_estimate=pl.CostEstimate(
            flops=count * 6 * tokens * width * width,
            bytes_accessed=count * 6 * tokens * width,
            transcendentals=0,
        ),
    )(*[near(x) for x in (*data[1:], *parts, *states)], *filled)


def swap(x, mask):
    count = lax.axis_size("seq")
    return lax.ppermute(x, "seq", [(i, i ^ mask) for i in range(count)])


def sliced_body(group):
    def body(queries, key_rows, value_rows, grad_out):
        count, index = lax.axis_size("seq"), lax.axis_index("seq")
        slots = group
        data = (queries, key_rows, value_rows, grad_out)

        came = swap(away_states(data, slots), 1)
        keep = keep_states(data, slots)
        *total, inner, outer = totals_of(came, keep)

        held = [total[0]] + [swap(total[j], 2 * j) for j in range(1, group)]
        parts = local_parts(data, total[0])

        block = block_sum(held, parts[0])
        keys, rests = block[0], block[1]
        carry = jnp.zeros_like(block)
        bit = 2 * group
        while bit < count:
            upper = (index & bit) != 0
            if 2 * bit < count:
                got = swap(jnp.stack([keys, rests]), bit)
                keys, rests = keys + got[0], rests + got[1]
                got_keys, got_rests = got[0], got[1]
            else:
                got_keys = got_rests = swap(jnp.where(upper, rests, keys), bit)
            carry = carry + jnp.stack(
                [jnp.where(upper, got_keys, 0.0), jnp.where(upper, 0.0, got_rests)]
            )
            bit *= 2

        around = [outside_of(carry, held, j) for j in range(group)]
        around = [swap(x, 2 * j) if j else x for j, x in enumerate(around)]
        soon, late = (0, group - 1), tuple(range(group - 2, 0, -1))
        mine, theirs = shares_of(inner, outer, around, soon)
        other = swap(theirs, 1)
        *done, mark = final_sums(data, parts, [mine], [(False, soon)])
        late_mine, late_theirs = shares_of(inner, outer, around, late, [mark])
        late_other = swap(late_theirs, 1)
        pieces = [(True, soon), (False, late)]
        done = final_sums(data, parts, [other, late_mine], pieces, done)
        return tuple(final_sums(data, parts, [late_other], [(True, late)], done))

    return body


def solution(mesh):
    count = mesh.shape["seq"]

    def run(queries, key_rows, value_rows, grad_out):
        heads = queries.shape[0] // mesh.shape["head"]
        tokens = queries.shape[1] // count
        group = heads // 2
        powers = all(n > 0 and n & (n - 1) == 0 for n in (count, group))
        fits = powers and heads == 2 * group and tokens == TILE and count >= 4 * group
        body = sliced_body(group) if fits else plain_body
        return jax.shard_map(
            body, mesh=mesh, in_specs=(SPEC,) * 4, out_specs=(SPEC,) * 3, check_vma=False
        )(queries, key_rows, value_rows, grad_out)

    return run
```

```python
import functools

import jax
import jax.numpy as jnp
from jax import lax
from jax.experimental import pallas as pl
from jax.experimental.pallas import tpu as pltpu
from jax.sharding import PartitionSpec as P

TILE = 256
SPEC = P("head", "seq", None)
F32 = jnp.float32
BF16 = jnp.bfloat16


def entering(x, axis, combine, identity, reverse):
    count, place = (lax.axis_size(axis), lax.axis_index(axis))
    everything = lax.all_gather(x, axis)
    start = jnp.broadcast_to(jnp.asarray(identity, x.dtype), x.shape)

    def turn(k, before):
        at = count - 1 - k if reverse else k
        reached = at > place if reverse else at < place
        new = combine(before, everything[at])
        return jnp.where(reached, new, before)

    return lax.fori_loop(0, count, turn, start)


def add_states(earlier, latter):
    return earlier + latter


def plain_body(queries, key_rows, value_rows, grad_out):
    head_count, tokens, head_width = queries.shape
    tile_count = tokens // TILE
    tile_shape = (head_count, tile_count, TILE, head_width)
    query_tiles = queries.reshape(tile_shape)
    key_tiles = key_rows.reshape(tile_shape)
    value_tiles = value_rows.reshape(tile_shape)
    grad_tiles = grad_out.reshape(tile_shape)

    def product(rule, a, b):
        return jnp.einsum(rule, a, b, preferred_element_type=F32)

    key_state = product("hjsa,hjsb->hjab", key_tiles, value_tiles)
    query_state = product("hjta,hjtb->hjab", query_tiles, grad_tiles)
    local_keys = jnp.sum(key_state, 1)
    local_queries = jnp.sum(query_state, 1)
    blank_state = jnp.zeros_like(local_keys)
    incoming = entering(local_keys, "seq", add_states, blank_state, False)
    outgoing = entering(local_queries, "seq", add_states, blank_state, True)
    zero_state = jnp.zeros((head_count, 1, head_width, head_width), F32)
    earlier_states = incoming[:, None] + jnp.concatenate(
        [zero_state, jnp.cumsum(key_state, 1)[:, :-1]], 1
    )
    later_states = outgoing[:, None] + jnp.concatenate(
        [jnp.cumsum(query_state[:, ::-1], 1)[:, ::-1][:, 1:], zero_state], 1
    )
    earlier_states = earlier_states.astype(BF16)
    later_states = later_states.astype(BF16)
    causal = (jnp.arange(TILE)[:, None] >= jnp.arange(TILE)[None, :])[None, None]
    out_scores = product("hjta,hjsa->hjts", grad_tiles, value_tiles)
    out_scores = jnp.where(causal, out_scores, 0.0).astype(BF16)
    attn_scores = product("hjta,hjsa->hjts", query_tiles, key_tiles)
    attn_scores = jnp.where(causal, attn_scores, 0.0).astype(BF16)
    grad_query = product("hjts,hjsa->hjta", out_scores, key_tiles)
    grad_query = grad_query + product("hjtb,hjab->hjta", grad_tiles, earlier_states)
    grad_key = product("hjts,hjta->hjsa", out_scores, query_tiles)
    grad_key = grad_key + product("hjsb,hjab->hjsa", value_tiles, later_states)
    grad_value = product("hjts,hjtb->hjsb", attn_scores, grad_tiles)
    grad_value = grad_value + product("hjsa,hjab->hjsb", key_tiles, later_states)
    flat_shape = (head_count, tokens, head_width)
    return tuple(
        x.astype(BF16).reshape(flat_shape) for x in (grad_query, grad_key, grad_value)
    )


WHOLE = pl.BlockSpec(memory_space=pltpu.VMEM)
PLACED = pl.BlockSpec(memory_space=pl.ANY)
FAR = pl.BlockSpec(memory_space=pltpu.HBM)
ROOM = pltpu.CompilerParams(vmem_limit_bytes=16 * 2**20)


def near(x):
    return pltpu.with_memory_space_constraint(x, pltpu.VMEM)


def far(x):
    return pltpu.with_memory_space_constraint(x, pltpu.HBM)


def dot(a, b, da, db):
    return lax.dot_general(a, b, (((da,), (db,)), ((), ())), preferred_element_type=F32)


def place_of(slots):
    index = lax.axis_index("seq")
    return index & 1, (index >> 1) & (slots - 1)


def states_into(outs, split, m, a, b, first, rank):
    for out, part in zip(outs, split):
        for n, slot in enumerate(part):
            head = first + (rank ^ slot)
            out[n, m] = dot(a[head], b[head], 0, 0)


def away_kernel(q, k, v, g, *refs, split):
    *outs, qs, ks, vs, gs, sems = refs
    slots = qs.shape[0]
    core, rank = place_of(slots)
    first = (1 - core) * slots
    copies = []
    for n, (there, here) in enumerate(((k, ks), (v, vs), (q, qs), (g, gs))):
        copies.append(pltpu.make_async_copy(there.at[pl.ds(first, slots)], here, sems.at[n]))
        copies[-1].start()
    copies[0].wait()
    copies[1].wait()
    states_into(outs, split, 0, ks, vs, 0, rank)
    copies[2].wait()
    copies[3].wait()
    states_into(outs, split, 1, qs, gs, 0, rank)


def keep_kernel(q, k, v, g, *outs, split):
    slots = q.shape[0] // 2
    core, rank = place_of(slots)
    states_into(outs, split, 0, k, v, core * slots, rank)
    states_into(outs, split, 1, q, g, core * slots, rank)


def state_call(kernel, data, split, place, spec, scratch):
    heads, tokens, width = data[0].shape
    return pl.pallas_call(
        functools.partial(kernel, split=split),
        out_shape=[pltpu.VMEM((len(part), 2, width, width), F32) for part in split],
        in_specs=[spec] * 4,
        out_specs=[WHOLE] * len(split),
        scratch_shapes=scratch,
        compiler_params=ROOM,
        cost_estimate=pl.CostEstimate(
            flops=heads * 2 * tokens * width * width,
            bytes_accessed=heads * 4 * tokens * width,
            transcendentals=0,
        ),
    )(*[place(x) for x in data])


def away_states(data, slots, split):
    _, tokens, width = data[0].shape
    scratch = [pltpu.VMEM((slots, tokens, width), BF16)] * 4 + [pltpu.SemaphoreType.DMA((4,))]
    return state_call(away_kernel, data, split, far, FAR, scratch)


def keep_states(data, slots, split):
    return state_call(keep_kernel, data, split, near, WHOLE, [])


def total_kernel(came, keep, *refs):
    *totals, inner, outer = refs
    core = lax.axis_index("seq") & 1
    for i, out in enumerate(totals):
        out[...] = came[i] + keep[i]
        inner[i] = jnp.where(core == 0, came[i, 1], came[i, 0])
        outer[i] = jnp.where(core == 0, keep[i, 0], keep[i, 1])


def totals_of(came, keep):
    slots, _, width, _ = keep.shape
    return pl.pallas_call(
        total_kernel,
        out_shape=[pltpu.VMEM((2, width, width), F32)] * slots
        + [pltpu.VMEM((slots, width, width), F32)] * 2,
        in_specs=[WHOLE] * 2,
        out_specs=[WHOLE] * (slots + 2),
        compiler_params=ROOM,
    )(near(came), near(keep))


def outside_kernel(carry, *refs, slot, group):
    out = refs[-1]
    _, rank = place_of(group)
    earlier, later = carry[0], carry[1]
    for i in range(group):
        if i != slot:
            before = (rank ^ i) < (rank ^ slot)
            earlier = earlier + jnp.where(before, refs[i][0], 0.0)
            later = later + jnp.where(before, 0.0, refs[i][1])
    out[0] = earlier
    out[1] = later


def outside_of(carry, held, slot):
    return pl.pallas_call(
        functools.partial(outside_kernel, slot=slot, group=len(held)),
        out_shape=pltpu.VMEM(carry.shape, F32),
        in_specs=[WHOLE] * (1 + len(held)),
        out_specs=WHOLE,
        compiler_params=ROOM,
    )(near(carry), *[near(x) for x in held])


def share_kernel(*refs, rows):
    mine, theirs = refs[-2:]
    first = lax.axis_index("seq") & 1 == 0
    for n, i in enumerate(rows):
        inner, outer, around = refs[3 * n : 3 * n + 3]
        earlier, later = around[0], around[1]
        mine[n, 0] = earlier + jnp.where(first, 0.0, inner[i])
        mine[n, 1] = later + jnp.where(first, inner[i], 0.0)
        theirs[n, 0] = earlier + jnp.where(first, outer[i], 0.0)
        theirs[n, 1] = later + jnp.where(first, 0.0, outer[i])


def shares_of(inner, outer, around, slots, after=()):
    shape = (len(slots), *around[0].shape)
    given = [x for i in slots for x in (inner[i][0], outer[i][0], around[i])]
    return pl.pallas_call(
        functools.partial(share_kernel, rows=[inner[i][1] for i in slots]),
        out_shape=[pltpu.VMEM(shape, F32)] * 2,
        in_specs=[WHOLE] * len(given) + [PLACED] * len(after),
        out_specs=[WHOLE] * 2,
        compiler_params=ROOM,
    )(*[near(x) for x in (*given, *after)])


def local_kernel(qs, ks, vs, gs, after, gq, gk, gv):
    heads, tokens, _ = qs.shape
    row = lax.broadcasted_iota(jnp.int32, (tokens, tokens), 0)
    col = lax.broadcasted_iota(jnp.int32, (tokens, tokens), 1)
    for i in range(heads):
        q, k, v, g = qs[i], ks[i], vs[i], gs[i]
        score = jnp.where(row >= col, dot(g, v, 1, 1), 0.0).astype(BF16)
        gq[i] = dot(score, k, 1, 0)
        score = jnp.where(row <= col, dot(v, g, 1, 1), 0.0).astype(BF16)
        gk[i] = dot(score, q, 1, 0)
        score = jnp.where(row <= col, dot(k, q, 1, 1), 0.0).astype(BF16)
        gv[i] = dot(score, g, 1, 0)


def local_parts(data, after):
    heads, tokens, width = data[0].shape
    return pl.pallas_call(
        local_kernel,
        out_shape=[pltpu.VMEM(data[0].shape, F32)] * 3,
        in_specs=[WHOLE] * 4 + [PLACED],
        out_specs=[WHOLE] * 3,
        compiler_params=ROOM,
        cost_estimate=pl.CostEstimate(
            flops=heads * 12 * tokens * tokens * width,
            bytes_accessed=heads * 20 * tokens * width,
            transcendentals=0,
        ),
    )(*[near(x) for x in data], near(after))


def block_kernel(after, *refs):
    out = refs[-1]
    total = refs[0][...]
    for x in refs[1:-1]:
        total = total + x[...]
    out[...] = total


def block_sum(held, after):
    return pl.pallas_call(
        block_kernel,
        out_shape=pltpu.VMEM(held[0].shape, F32),
        in_specs=[PLACED] + [WHOLE] * len(held),
        out_specs=WHOLE,
        compiler_params=ROOM,
    )(near(after), *[near(x) for x in held])


def final_kernel(k, v, g, lq, lk, lv, *refs, pieces, given):
    bq, bk, bv, sems = refs[-4:]
    gq, gk, gv, *marks = refs[len(pieces) + given : -4]
    for mark in marks:
        mark[...] = jnp.zeros_like(mark)
    half = k.shape[0] // 2
    core, rank = place_of(half)
    copies = []
    for state, (other, slots) in zip(refs, pieces):
        first = (1 - core if other else core) * half
        for i, slot in enumerate(slots):
            earlier, later = state[i, 0].astype(BF16), state[i, 1].astype(BF16)
            head, n = first + (rank ^ slot), len(copies) // 3
            bq[n] = (lq[head] + dot(g[head], earlier, 1, 1)).astype(BF16)
            bk[n] = (lk[head] + dot(v[head], later, 1, 1)).astype(BF16)
            bv[n] = (lv[head] + dot(k[head], later, 1, 0)).astype(BF16)
            for m, (here, there) in enumerate(((bq, gq), (bk, gk), (bv, gv))):
                copies.append(pltpu.make_async_copy(here.at[n], there.at[head], sems.at[n, m]))
                copies[-1].start()
    for copy in copies:
        copy.wait()


def final_sums(data, parts, states, pieces, filled=()):
    _, tokens, width = data[0].shape
    count = sum(len(slots) for _, slots in pieces)
    held = 6 + len(states)
    return pl.pallas_call(
        functools.partial(final_kernel, pieces=pieces, given=len(filled)),
        out_shape=[jax.ShapeDtypeStruct(data[0].shape, BF16)] * 3
        + [pltpu.VMEM((8, width), F32)] * (not filled),
        in_specs=[WHOLE] * held + [PLACED] * len(filled),
        out_specs=[PLACED] * 3 + [WHOLE] * (not filled),
        input_output_aliases={held + n: n for n in range(len(filled))},
        scratch_shapes=[pltpu.VMEM((count, tokens, width), BF16)] * 3
        + [pltpu.SemaphoreType.DMA((count, 3))],
        compiler_params=ROOM,
        cost_estimate=pl.CostEstimate(
            flops=count * 6 * tokens * width * width,
            bytes_accessed=count * 6 * tokens * width,
            transcendentals=0,
        ),
    )(*[near(x) for x in (*data[1:], *parts, *states)], *filled)


def swap(x, mask):
    count = lax.axis_size("seq")
    return lax.ppermute(x, "seq", [(i, i ^ mask) for i in range(count)])


def sliced_body(group):
    def body(queries, key_rows, value_rows, grad_out):
        count, index = lax.axis_size("seq"), lax.axis_index("seq")
        slots = group
        data = (queries, key_rows, value_rows, grad_out)

        split = ((1, 2), (0, *range(3, slots)))
        away = away_states(data, slots, split)
        keep = keep_states(data, slots, split)
        came = [swap(x, 1) for x in away]
        total, inner, outer = {}, {}, {}
        for part, a, b in zip(split, came, keep):
            *sums, into, from_here = totals_of(a, b)
            for n, j in enumerate(part):
                total[j], inner[j], outer[j] = sums[n], (into, n), (from_here, n)

        held = [total[0]] + [swap(total[j], 2 * j) for j in range(1, group)]
        parts = local_parts(data, total[0])

        block = block_sum(held, parts[0])
        keys, rests = block[0], block[1]
        carry = jnp.zeros_like(block)
        bit = 2 * group
        while bit < count:
            upper = (index & bit) != 0
            if 2 * bit < count:
                got = swap(jnp.stack([keys, rests]), bit)
                keys, rests = keys + got[0], rests + got[1]
                got_keys, got_rests = got[0], got[1]
            else:
                got_keys = got_rests = swap(jnp.where(upper, rests, keys), bit)
            carry = carry + jnp.stack(
                [jnp.where(upper, got_keys, 0.0), jnp.where(upper, 0.0, got_rests)]
            )
            bit *= 2

        around = [outside_of(carry, held, j) for j in range(group)]
        around = [swap(x, 2 * j) if j else x for j, x in enumerate(around)]
        soon, late = (0, group - 1), tuple(range(group - 2, 0, -1))
        mine, theirs = shares_of(inner, outer, around, soon)
        other = swap(theirs, 1)
        *done, mark = final_sums(data, parts, [mine], [(False, soon)])
        late_mine, late_theirs = shares_of(inner, outer, around, late, [mark])
        late_other = swap(late_theirs, 1)
        pieces = [(True, soon), (False, late)]
        done = final_sums(data, parts, [other, late_mine], pieces, done)
        return tuple(final_sums(data, parts, [late_other], [(True, late)], done))

    return body


def solution(mesh):
    count = mesh.shape["seq"]

    def run(queries, key_rows, value_rows, grad_out):
        heads = queries.shape[0] // mesh.shape["head"]
        tokens = queries.shape[1] // count
        group = heads // 2
        powers = all(n > 0 and n & (n - 1) == 0 for n in (count, group))
        fits = powers and heads == 2 * group and group >= 4 and tokens == TILE and count >= 4 * group
        body = sliced_body(group) if fits else plain_body
        return jax.shard_map(
            body, mesh=mesh, in_specs=(SPEC,) * 4, out_specs=(SPEC,) * 3, check_vma=False
        )(queries, key_rows, value_rows, grad_out)

    return run
```

```python
import functools

import jax
import jax.numpy as jnp
from jax import lax
from jax.experimental import pallas as pl
from jax.experimental.pallas import tpu as pltpu
from jax.sharding import PartitionSpec as P

TILE = 256
SPEC = P("head", "seq", None)
F32 = jnp.float32
BF16 = jnp.bfloat16


def entering(x, axis, combine, identity, reverse):
    count, place = (lax.axis_size(axis), lax.axis_index(axis))
    everything = lax.all_gather(x, axis)
    start = jnp.broadcast_to(jnp.asarray(identity, x.dtype), x.shape)

    def turn(k, before):
        at = count - 1 - k if reverse else k
        reached = at > place if reverse else at < place
        new = combine(before, everything[at])
        return jnp.where(reached, new, before)

    return lax.fori_loop(0, count, turn, start)


def add_states(earlier, latter):
    return earlier + latter


def plain_body(queries, key_rows, value_rows, grad_out):
    head_count, tokens, head_width = queries.shape
    tile_count = tokens // TILE
    tile_shape = (head_count, tile_count, TILE, head_width)
    query_tiles = queries.reshape(tile_shape)
    key_tiles = key_rows.reshape(tile_shape)
    value_tiles = value_rows.reshape(tile_shape)
    grad_tiles = grad_out.reshape(tile_shape)

    def product(rule, a, b):
        return jnp.einsum(rule, a, b, preferred_element_type=F32)

    key_state = product("hjsa,hjsb->hjab", key_tiles, value_tiles)
    query_state = product("hjta,hjtb->hjab", query_tiles, grad_tiles)
    local_keys = jnp.sum(key_state, 1)
    local_queries = jnp.sum(query_state, 1)
    blank_state = jnp.zeros_like(local_keys)
    incoming = entering(local_keys, "seq", add_states, blank_state, False)
    outgoing = entering(local_queries, "seq", add_states, blank_state, True)
    zero_state = jnp.zeros((head_count, 1, head_width, head_width), F32)
    earlier_states = incoming[:, None] + jnp.concatenate(
        [zero_state, jnp.cumsum(key_state, 1)[:, :-1]], 1
    )
    later_states = outgoing[:, None] + jnp.concatenate(
        [jnp.cumsum(query_state[:, ::-1], 1)[:, ::-1][:, 1:], zero_state], 1
    )
    earlier_states = earlier_states.astype(BF16)
    later_states = later_states.astype(BF16)
    causal = (jnp.arange(TILE)[:, None] >= jnp.arange(TILE)[None, :])[None, None]
    out_scores = product("hjta,hjsa->hjts", grad_tiles, value_tiles)
    out_scores = jnp.where(causal, out_scores, 0.0).astype(BF16)
    attn_scores = product("hjta,hjsa->hjts", query_tiles, key_tiles)
    attn_scores = jnp.where(causal, attn_scores, 0.0).astype(BF16)
    grad_query = product("hjts,hjsa->hjta", out_scores, key_tiles)
    grad_query = grad_query + product("hjtb,hjab->hjta", grad_tiles, earlier_states)
    grad_key = product("hjts,hjta->hjsa", out_scores, query_tiles)
    grad_key = grad_key + product("hjsb,hjab->hjsa", value_tiles, later_states)
    grad_value = product("hjts,hjtb->hjsb", attn_scores, grad_tiles)
    grad_value = grad_value + product("hjsa,hjab->hjsb", key_tiles, later_states)
    flat_shape = (head_count, tokens, head_width)
    return tuple(
        x.astype(BF16).reshape(flat_shape) for x in (grad_query, grad_key, grad_value)
    )


WHOLE = pl.BlockSpec(memory_space=pltpu.VMEM)
PLACED = pl.BlockSpec(memory_space=pl.ANY)
FAR = pl.BlockSpec(memory_space=pltpu.HBM)
ROOM = pltpu.CompilerParams(vmem_limit_bytes=16 * 2**20)


def near(x):
    return pltpu.with_memory_space_constraint(x, pltpu.VMEM)


def far(x):
    return pltpu.with_memory_space_constraint(x, pltpu.HBM)


def dot(a, b, da, db):
    return lax.dot_general(a, b, (((da,), (db,)), ((), ())), preferred_element_type=F32)


def place_of(slots):
    index = lax.axis_index("seq")
    return index & 1, (index >> 1) & (slots - 1)


def away_kernel(q, k, v, g, out, qs, ks, vs, gs, sems, *, part):
    slots = q.shape[0] // 2
    core, rank = place_of(slots)
    first = (1 - core) * slots
    copies = []
    for n, (there, here) in enumerate(((k, ks), (v, vs), (q, qs), (g, gs))):
        for m, slot in enumerate(part):
            head = first + (rank ^ slot)
            copies.append(pltpu.make_async_copy(there.at[head], here.at[m], sems.at[n, m]))
            copies[-1].start()
    for copy in copies:
        copy.wait()
    for m in range(len(part)):
        out[m, 0] = dot(ks[m], vs[m], 0, 0)
        out[m, 1] = dot(qs[m], gs[m], 0, 0)


def near_kernel(q, k, v, g, *outs, parts, other):
    slots = q.shape[0] // 2
    core, rank = place_of(slots)
    first = (1 - core if other else core) * slots
    for out, part in zip(outs, parts):
        for m, slot in enumerate(part):
            head = first + (rank ^ slot)
            out[m, 0] = dot(k[head], v[head], 0, 0)
            out[m, 1] = dot(q[head], g[head], 0, 0)


def state_call(kernel, data, parts, place, spec, scratch):
    _, tokens, width = data[0].shape
    count = sum(len(part) for part in parts)
    return pl.pallas_call(
        kernel,
        out_shape=[pltpu.VMEM((len(part), 2, width, width), F32) for part in parts],
        in_specs=[spec] * 4,
        out_specs=[WHOLE] * len(parts),
        scratch_shapes=scratch,
        compiler_params=ROOM,
        cost_estimate=pl.CostEstimate(
            flops=count * 4 * tokens * width * width,
            bytes_accessed=count * 8 * tokens * width,
            transcendentals=0,
        ),
    )(*[place(x) for x in data])


def away_states(data, part):
    _, tokens, width = data[0].shape
    scratch = [pltpu.VMEM((len(part), tokens, width), BF16)] * 4
    scratch.append(pltpu.SemaphoreType.DMA((4, len(part))))
    kernel = functools.partial(away_kernel, part=part)
    return state_call(kernel, data, [part], far, FAR, scratch)


def near_states(data, parts, other):
    kernel = functools.partial(near_kernel, parts=parts, other=other)
    return state_call(kernel, data, parts, near, WHOLE, [])


def total_kernel(came, keep, *refs):
    *totals, inner, outer = refs
    core = lax.axis_index("seq") & 1
    for i, out in enumerate(totals):
        out[...] = came[i] + keep[i]
        inner[i] = jnp.where(core == 0, came[i, 1], came[i, 0])
        outer[i] = jnp.where(core == 0, keep[i, 0], keep[i, 1])


def totals_of(came, keep):
    slots, _, width, _ = keep.shape
    return pl.pallas_call(
        total_kernel,
        out_shape=[pltpu.VMEM((2, width, width), F32)] * slots
        + [pltpu.VMEM((slots, width, width), F32)] * 2,
        in_specs=[WHOLE] * 2,
        out_specs=[WHOLE] * (slots + 2),
        compiler_params=ROOM,
    )(near(came), near(keep))


def outside_kernel(after, carry, *refs, slot, group):
    out = refs[-1]
    _, rank = place_of(group)
    earlier, later = carry[0], carry[1]
    for i in range(group):
        if i != slot:
            before = (rank ^ i) < (rank ^ slot)
            earlier = earlier + jnp.where(before, refs[i][0], 0.0)
            later = later + jnp.where(before, 0.0, refs[i][1])
    out[0] = earlier
    out[1] = later


def outside_of(carry, held, slot, after):
    return pl.pallas_call(
        functools.partial(outside_kernel, slot=slot, group=len(held)),
        out_shape=pltpu.VMEM(carry.shape, F32),
        in_specs=[PLACED] + [WHOLE] * (1 + len(held)),
        out_specs=WHOLE,
        compiler_params=ROOM,
    )(near(after), near(carry), *[near(x) for x in held])


def share_kernel(*refs, rows):
    mine, theirs = refs[-2:]
    first = lax.axis_index("seq") & 1 == 0
    for n, i in enumerate(rows):
        inner, outer, around = refs[3 * n : 3 * n + 3]
        earlier, later = around[0], around[1]
        mine[n, 0] = earlier + jnp.where(first, 0.0, inner[i])
        mine[n, 1] = later + jnp.where(first, inner[i], 0.0)
        theirs[n, 0] = earlier + jnp.where(first, outer[i], 0.0)
        theirs[n, 1] = later + jnp.where(first, 0.0, outer[i])


def shares_of(inner, outer, around, slots, after=()):
    shape = (len(slots), *around[0].shape)
    given = [x for i in slots for x in (inner[i][0], outer[i][0], around[i])]
    return pl.pallas_call(
        functools.partial(share_kernel, rows=[inner[i][1] for i in slots]),
        out_shape=[pltpu.VMEM(shape, F32)] * 2,
        in_specs=[WHOLE] * len(given) + [PLACED] * len(after),
        out_specs=[WHOLE] * 2,
        compiler_params=ROOM,
    )(*[near(x) for x in (*given, *after)])


def local_kernel(qs, ks, vs, gs, after, gq, gk, gv):
    heads, tokens, _ = qs.shape
    row = lax.broadcasted_iota(jnp.int32, (tokens, tokens), 0)
    col = lax.broadcasted_iota(jnp.int32, (tokens, tokens), 1)
    for i in range(heads):
        q, k, v, g = qs[i], ks[i], vs[i], gs[i]
        score = jnp.where(row >= col, dot(g, v, 1, 1), 0.0).astype(BF16)
        gq[i] = dot(score, k, 1, 0)
        score = jnp.where(row <= col, dot(v, g, 1, 1), 0.0).astype(BF16)
        gk[i] = dot(score, q, 1, 0)
        score = jnp.where(row <= col, dot(k, q, 1, 1), 0.0).astype(BF16)
        gv[i] = dot(score, g, 1, 0)


def local_parts(data, after):
    heads, tokens, width = data[0].shape
    return pl.pallas_call(
        local_kernel,
        out_shape=[pltpu.VMEM(data[0].shape, F32)] * 3,
        in_specs=[WHOLE] * 4 + [PLACED],
        out_specs=[WHOLE] * 3,
        compiler_params=ROOM,
        cost_estimate=pl.CostEstimate(
            flops=heads * 12 * tokens * tokens * width,
            bytes_accessed=heads * 20 * tokens * width,
            transcendentals=0,
        ),
    )(*[near(x) for x in data], near(after))


def block_kernel(*refs):
    out = refs[-1]
    total = refs[0][...]
    for x in refs[1:-1]:
        total = total + x[...]
    out[...] = total


def block_sum(held):
    return pl.pallas_call(
        block_kernel,
        out_shape=pltpu.VMEM(held[0].shape, F32),
        in_specs=[WHOLE] * len(held),
        out_specs=WHOLE,
        compiler_params=ROOM,
    )(*[near(x) for x in held])


def final_kernel(k, v, g, lq, lk, lv, *refs, pieces, given):
    bq, bk, bv, sems = refs[-4:]
    gq, gk, gv, *marks = refs[len(pieces) + given : -4]
    for mark in marks:
        mark[...] = jnp.zeros_like(mark)
    half = k.shape[0] // 2
    core, rank = place_of(half)
    copies = []
    for state, (other, slots) in zip(refs, pieces):
        first = (1 - core if other else core) * half
        for i, slot in enumerate(slots):
            earlier, later = state[i, 0].astype(BF16), state[i, 1].astype(BF16)
            head, n = first + (rank ^ slot), len(copies) // 3
            bq[n] = (lq[head] + dot(g[head], earlier, 1, 1)).astype(BF16)
            bk[n] = (lk[head] + dot(v[head], later, 1, 1)).astype(BF16)
            bv[n] = (lv[head] + dot(k[head], later, 1, 0)).astype(BF16)
            for m, (here, there) in enumerate(((bq, gq), (bk, gk), (bv, gv))):
                copies.append(pltpu.make_async_copy(here.at[n], there.at[head], sems.at[n, m]))
                copies[-1].start()
    for copy in copies:
        copy.wait()


def final_sums(data, parts, states, pieces, filled=()):
    _, tokens, width = data[0].shape
    count = sum(len(slots) for _, slots in pieces)
    held = 6 + len(states)
    return pl.pallas_call(
        functools.partial(final_kernel, pieces=pieces, given=len(filled)),
        out_shape=[jax.ShapeDtypeStruct(data[0].shape, BF16)] * 3
        + [pltpu.VMEM((8, width), F32)] * (not filled),
        in_specs=[WHOLE] * held + [PLACED] * len(filled),
        out_specs=[PLACED] * 3 + [WHOLE] * (not filled),
        input_output_aliases={held + n: n for n in range(len(filled))},
        scratch_shapes=[pltpu.VMEM((count, tokens, width), BF16)] * 3
        + [pltpu.SemaphoreType.DMA((count, 3))],
        compiler_params=ROOM,
        cost_estimate=pl.CostEstimate(
            flops=count * 6 * tokens * width * width,
            bytes_accessed=count * 6 * tokens * width,
            transcendentals=0,
        ),
    )(*[near(x) for x in (*data[1:], *parts, *states)], *filled)


def swap(x, mask):
    count = lax.axis_size("seq")
    return lax.ppermute(x, "seq", [(i, i ^ mask) for i in range(count)])


def sliced_body(group):
    def body(queries, key_rows, value_rows, grad_out):
        count, index = lax.axis_size("seq"), lax.axis_index("seq")
        slots = group
        data = (queries, key_rows, value_rows, grad_out)

        split = ((1, 2), (0, *range(3, slots)))
        away = away_states(data, split[0]) + near_states(data, split[1:], True)
        keep = near_states(data, split, False)
        came = [swap(x, 1) for x in away]
        total, inner, outer = {}, {}, {}
        for part, a, b in zip(split, came, keep):
            *sums, into, from_here = totals_of(a, b)
            for n, j in enumerate(part):
                total[j], inner[j], outer[j] = sums[n], (into, n), (from_here, n)

        held = [total[0]] + [swap(total[j], 2 * j) for j in range(1, group)]

        block = block_sum(held)
        parts = local_parts(data, block)
        keys, rests = block[0], block[1]
        carry = jnp.zeros_like(block)
        bit = 2 * group
        while bit < count:
            upper = (index & bit) != 0
            if 2 * bit < count:
                got = swap(jnp.stack([keys, rests]), bit)
                keys, rests = keys + got[0], rests + got[1]
                got_keys, got_rests = got[0], got[1]
            else:
                got_keys = got_rests = swap(jnp.where(upper, rests, keys), bit)
            carry = carry + jnp.stack(
                [jnp.where(upper, got_keys, 0.0), jnp.where(upper, 0.0, got_rests)]
            )
            bit *= 2

        around = [outside_of(carry, held, j, parts[0]) for j in range(group)]
        around = [swap(x, 2 * j) if j else x for j, x in enumerate(around)]
        soon, late = (0, group - 1), tuple(range(group - 2, 0, -1))
        mine, theirs = shares_of(inner, outer, around, soon)
        other = swap(theirs, 1)
        *done, mark = final_sums(data, parts, [mine], [(False, soon)])
        late_mine, late_theirs = shares_of(inner, outer, around, late, [mark])
        late_other = swap(late_theirs, 1)
        pieces = [(True, soon), (False, late)]
        done = final_sums(data, parts, [other, late_mine], pieces, done)
        return tuple(final_sums(data, parts, [late_other], [(True, late)], done))

    return body


def solution(mesh):
    count = mesh.shape["seq"]

    def run(queries, key_rows, value_rows, grad_out):
        heads = queries.shape[0] // mesh.shape["head"]
        tokens = queries.shape[1] // count
        group = heads // 2
        powers = all(n > 0 and n & (n - 1) == 0 for n in (count, group))
        fits = powers and heads == 2 * group and group >= 4 and tokens == TILE and count >= 4 * group
        body = sliced_body(group) if fits else plain_body
        return jax.shard_map(
            body, mesh=mesh, in_specs=(SPEC,) * 4, out_specs=(SPEC,) * 3, check_vma=False
        )(queries, key_rows, value_rows, grad_out)

    return run
```

```python
import functools

import jax
import jax.numpy as jnp
from jax import lax
from jax.experimental import pallas as pl
from jax.experimental.pallas import tpu as pltpu
from jax.sharding import PartitionSpec as P

TILE = 256
SPEC = P("head", "seq", None)
F32 = jnp.float32
BF16 = jnp.bfloat16


def entering(x, axis, combine, identity, reverse):
    count, place = (lax.axis_size(axis), lax.axis_index(axis))
    everything = lax.all_gather(x, axis)
    start = jnp.broadcast_to(jnp.asarray(identity, x.dtype), x.shape)

    def turn(k, before):
        at = count - 1 - k if reverse else k
        reached = at > place if reverse else at < place
        new = combine(before, everything[at])
        return jnp.where(reached, new, before)

    return lax.fori_loop(0, count, turn, start)


def add_states(earlier, latter):
    return earlier + latter


def plain_body(queries, key_rows, value_rows, grad_out):
    head_count, tokens, head_width = queries.shape
    tile_count = tokens // TILE
    tile_shape = (head_count, tile_count, TILE, head_width)
    query_tiles = queries.reshape(tile_shape)
    key_tiles = key_rows.reshape(tile_shape)
    value_tiles = value_rows.reshape(tile_shape)
    grad_tiles = grad_out.reshape(tile_shape)

    def product(rule, a, b):
        return jnp.einsum(rule, a, b, preferred_element_type=F32)

    key_state = product("hjsa,hjsb->hjab", key_tiles, value_tiles)
    query_state = product("hjta,hjtb->hjab", query_tiles, grad_tiles)
    local_keys = jnp.sum(key_state, 1)
    local_queries = jnp.sum(query_state, 1)
    blank_state = jnp.zeros_like(local_keys)
    incoming = entering(local_keys, "seq", add_states, blank_state, False)
    outgoing = entering(local_queries, "seq", add_states, blank_state, True)
    zero_state = jnp.zeros((head_count, 1, head_width, head_width), F32)
    earlier_states = incoming[:, None] + jnp.concatenate(
        [zero_state, jnp.cumsum(key_state, 1)[:, :-1]], 1
    )
    later_states = outgoing[:, None] + jnp.concatenate(
        [jnp.cumsum(query_state[:, ::-1], 1)[:, ::-1][:, 1:], zero_state], 1
    )
    earlier_states = earlier_states.astype(BF16)
    later_states = later_states.astype(BF16)
    causal = (jnp.arange(TILE)[:, None] >= jnp.arange(TILE)[None, :])[None, None]
    out_scores = product("hjta,hjsa->hjts", grad_tiles, value_tiles)
    out_scores = jnp.where(causal, out_scores, 0.0).astype(BF16)
    attn_scores = product("hjta,hjsa->hjts", query_tiles, key_tiles)
    attn_scores = jnp.where(causal, attn_scores, 0.0).astype(BF16)
    grad_query = product("hjts,hjsa->hjta", out_scores, key_tiles)
    grad_query = grad_query + product("hjtb,hjab->hjta", grad_tiles, earlier_states)
    grad_key = product("hjts,hjta->hjsa", out_scores, query_tiles)
    grad_key = grad_key + product("hjsb,hjab->hjsa", value_tiles, later_states)
    grad_value = product("hjts,hjtb->hjsb", attn_scores, grad_tiles)
    grad_value = grad_value + product("hjsa,hjab->hjsb", key_tiles, later_states)
    flat_shape = (head_count, tokens, head_width)
    return tuple(
        x.astype(BF16).reshape(flat_shape) for x in (grad_query, grad_key, grad_value)
    )


WHOLE = pl.BlockSpec(memory_space=pltpu.VMEM)
PLACED = pl.BlockSpec(memory_space=pl.ANY)
FAR = pl.BlockSpec(memory_space=pltpu.HBM)
ROOM = pltpu.CompilerParams(vmem_limit_bytes=16 * 2**20)


def near(x):
    return pltpu.with_memory_space_constraint(x, pltpu.VMEM)


def far(x):
    return pltpu.with_memory_space_constraint(x, pltpu.HBM)


def dot(a, b, da, db):
    return lax.dot_general(a, b, (((da,), (db,)), ((), ())), preferred_element_type=F32)


def turned(slot, group):
    return (group - slot) & (group - 1)


def place_of(group):
    index = lax.axis_index("seq")
    return index & 1, (index >> 1) & (group - 1)


def partner(core, rank, slot, group):
    return rank ^ (slot + core * (turned(slot, group) - slot))


def away_kernel(q, k, v, g, out, qs, ks, vs, gs, sems, *, part):
    slots = q.shape[0] // 2
    core, rank = place_of(slots)
    core = 1 - core
    copies = []
    for n, (there, here) in enumerate(((k, ks), (v, vs), (q, qs), (g, gs))):
        for m, slot in enumerate(part):
            head = core * slots + partner(core, rank, slot, slots)
            copies.append(pltpu.make_async_copy(there.at[head], here.at[m], sems.at[n, m]))
            copies[-1].start()
    for copy in copies:
        copy.wait()
    for m in range(len(part)):
        out[m, 0] = dot(ks[m], vs[m], 0, 0)
        out[m, 1] = dot(qs[m], gs[m], 0, 0)


def near_kernel(q, k, v, g, *outs, parts, other):
    slots = q.shape[0] // 2
    core, rank = place_of(slots)
    core = 1 - core if other else core
    for out, part in zip(outs, parts):
        for m, slot in enumerate(part):
            head = core * slots + partner(core, rank, slot, slots)
            out[m, 0] = dot(k[head], v[head], 0, 0)
            out[m, 1] = dot(q[head], g[head], 0, 0)


def state_call(kernel, data, parts, place, spec, scratch):
    _, tokens, width = data[0].shape
    count = sum(len(part) for part in parts)
    return pl.pallas_call(
        kernel,
        out_shape=[pltpu.VMEM((len(part), 2, width, width), F32) for part in parts],
        in_specs=[spec] * 4,
        out_specs=[WHOLE] * len(parts),
        scratch_shapes=scratch,
        compiler_params=ROOM,
        cost_estimate=pl.CostEstimate(
            flops=count * 4 * tokens * width * width,
            bytes_accessed=count * 8 * tokens * width,
            transcendentals=0,
        ),
    )(*[place(x) for x in data])


def away_states(data, part):
    _, tokens, width = data[0].shape
    scratch = [pltpu.VMEM((len(part), tokens, width), BF16)] * 4
    scratch.append(pltpu.SemaphoreType.DMA((4, len(part))))
    kernel = functools.partial(away_kernel, part=part)
    return state_call(kernel, data, [part], far, FAR, scratch)


def near_states(data, parts, other):
    kernel = functools.partial(near_kernel, parts=parts, other=other)
    return state_call(kernel, data, parts, near, WHOLE, [])


def total_kernel(came, keep, *refs):
    *totals, inner, outer = refs
    core = lax.axis_index("seq") & 1
    for i, out in enumerate(totals):
        out[...] = came[i] + keep[i]
        inner[i] = jnp.where(core == 0, came[i, 1], came[i, 0])
        outer[i] = jnp.where(core == 0, keep[i, 0], keep[i, 1])


def totals_of(came, keep):
    slots, _, width, _ = keep.shape
    return pl.pallas_call(
        total_kernel,
        out_shape=[pltpu.VMEM((2, width, width), F32)] * slots
        + [pltpu.VMEM((slots, width, width), F32)] * 2,
        in_specs=[WHOLE] * 2,
        out_specs=[WHOLE] * (slots + 2),
        compiler_params=ROOM,
    )(near(came), near(keep))


def outside_kernel(after, carry, *refs, slot, group):
    out = refs[-1]
    core, rank = place_of(group)
    earlier, later = carry[0], carry[1]
    there = partner(core, rank, slot, group)
    for i in range(group):
        if i != slot:
            before = partner(core, rank, i, group) < there
            earlier = earlier + jnp.where(before, refs[i][0], 0.0)
            later = later + jnp.where(before, 0.0, refs[i][1])
    out[0] = earlier
    out[1] = later


def outside_of(carry, held, slot, after):
    return pl.pallas_call(
        functools.partial(outside_kernel, slot=slot, group=len(held)),
        out_shape=pltpu.VMEM(carry.shape, F32),
        in_specs=[PLACED] + [WHOLE] * (1 + len(held)),
        out_specs=WHOLE,
        compiler_params=ROOM,
    )(near(after), near(carry), *[near(x) for x in held])


def share_kernel(*refs, rows):
    mine, theirs = refs[-2:]
    first = lax.axis_index("seq") & 1 == 0
    for n, i in enumerate(rows):
        inner, outer, around = refs[3 * n : 3 * n + 3]
        earlier, later = around[0], around[1]
        mine[n, 0] = earlier + jnp.where(first, 0.0, inner[i])
        mine[n, 1] = later + jnp.where(first, inner[i], 0.0)
        theirs[n, 0] = earlier + jnp.where(first, outer[i], 0.0)
        theirs[n, 1] = later + jnp.where(first, 0.0, outer[i])


def shares_of(inner, outer, around, slots, after=()):
    shape = (len(slots), *around[0].shape)
    given = [x for i in slots for x in (inner[i][0], outer[i][0], around[i])]
    return pl.pallas_call(
        functools.partial(share_kernel, rows=[inner[i][1] for i in slots]),
        out_shape=[pltpu.VMEM(shape, F32)] * 2,
        in_specs=[WHOLE] * len(given) + [PLACED] * len(after),
        out_specs=[WHOLE] * 2,
        compiler_params=ROOM,
    )(*[near(x) for x in (*given, *after)])


def local_kernel(qs, ks, vs, gs, after, gq, gk, gv):
    heads, tokens, _ = qs.shape
    row = lax.broadcasted_iota(jnp.int32, (tokens, tokens), 0)
    col = lax.broadcasted_iota(jnp.int32, (tokens, tokens), 1)
    for i in range(heads):
        q, k, v, g = qs[i], ks[i], vs[i], gs[i]
        score = jnp.where(row >= col, dot(g, v, 1, 1), 0.0).astype(BF16)
        gq[i] = dot(score, k, 1, 0)
        score = jnp.where(row <= col, dot(v, g, 1, 1), 0.0).astype(BF16)
        gk[i] = dot(score, q, 1, 0)
        score = jnp.where(row <= col, dot(k, q, 1, 1), 0.0).astype(BF16)
        gv[i] = dot(score, g, 1, 0)


def local_parts(data, after):
    heads, tokens, width = data[0].shape
    return pl.pallas_call(
        local_kernel,
        out_shape=[pltpu.VMEM(data[0].shape, F32)] * 3,
        in_specs=[WHOLE] * 4 + [PLACED],
        out_specs=[WHOLE] * 3,
        compiler_params=ROOM,
        cost_estimate=pl.CostEstimate(
            flops=heads * 12 * tokens * tokens * width,
            bytes_accessed=heads * 20 * tokens * width,
            transcendentals=0,
        ),
    )(*[near(x) for x in data], near(after))


def block_kernel(*refs):
    out = refs[-1]
    total = refs[0][...]
    for x in refs[1:-1]:
        total = total + x[...]
    out[...] = total


def block_sum(held):
    return pl.pallas_call(
        block_kernel,
        out_shape=pltpu.VMEM(held[0].shape, F32),
        in_specs=[WHOLE] * len(held),
        out_specs=WHOLE,
        compiler_params=ROOM,
    )(*[near(x) for x in held])


def final_kernel(k, v, g, lq, lk, lv, *refs, pieces, given):
    bq, bk, bv, sems = refs[-4:]
    gq, gk, gv, *marks = refs[len(pieces) + given : -4]
    for mark in marks:
        mark[...] = jnp.zeros_like(mark)
    half = k.shape[0] // 2
    core, rank = place_of(half)
    copies = []
    for state, (other, slots) in zip(refs, pieces):
        side = 1 - core if other else core
        for i, slot in enumerate(slots):
            earlier, later = state[i, 0].astype(BF16), state[i, 1].astype(BF16)
            head, n = side * half + partner(side, rank, slot, half), len(copies) // 3
            bq[n] = (lq[head] + dot(g[head], earlier, 1, 1)).astype(BF16)
            bk[n] = (lk[head] + dot(v[head], later, 1, 1)).astype(BF16)
            bv[n] = (lv[head] + dot(k[head], later, 1, 0)).astype(BF16)
            for m, (here, there) in enumerate(((bq, gq), (bk, gk), (bv, gv))):
                copies.append(pltpu.make_async_copy(here.at[n], there.at[head], sems.at[n, m]))
                copies[-1].start()
    for copy in copies:
        copy.wait()


def final_sums(data, parts, states, pieces, filled=()):
    _, tokens, width = data[0].shape
    count = sum(len(slots) for _, slots in pieces)
    held = 6 + len(states)
    return pl.pallas_call(
        functools.partial(final_kernel, pieces=pieces, given=len(filled)),
        out_shape=[jax.ShapeDtypeStruct(data[0].shape, BF16)] * 3
        + [pltpu.VMEM((8, width), F32)] * (not filled),
        in_specs=[WHOLE] * held + [PLACED] * len(filled),
        out_specs=[PLACED] * 3 + [WHOLE] * (not filled),
        input_output_aliases={held + n: n for n in range(len(filled))},
        scratch_shapes=[pltpu.VMEM((count, tokens, width), BF16)] * 3
        + [pltpu.SemaphoreType.DMA((count, 3))],
        compiler_params=ROOM,
        cost_estimate=pl.CostEstimate(
            flops=count * 6 * tokens * width * width,
            bytes_accessed=count * 6 * tokens * width,
            transcendentals=0,
        ),
    )(*[near(x) for x in (*data[1:], *parts, *states)], *filled)


def swap(x, mask):
    count = lax.axis_size("seq")
    return lax.ppermute(x, "seq", [(i, i ^ mask) for i in range(count)])


def swap_slot(x, slot, group):
    count = lax.axis_size("seq")
    masks = (2 * slot, 2 * turned(slot, group))
    return lax.ppermute(x, "seq", [(i, i ^ masks[i & 1]) for i in range(count)])


def sliced_body(group):
    def body(queries, key_rows, value_rows, grad_out):
        count, index = lax.axis_size("seq"), lax.axis_index("seq")
        slots = group
        data = (queries, key_rows, value_rows, grad_out)

        split = ((1, 2), (0, *range(3, slots)))
        away = away_states(data, split[0]) + near_states(data, split[1:], True)
        keep = near_states(data, split, False)
        came = [swap(x, 1) for x in away]
        total, inner, outer = {}, {}, {}
        for part, a, b in zip(split, came, keep):
            *sums, into, from_here = totals_of(a, b)
            for n, j in enumerate(part):
                total[j], inner[j], outer[j] = sums[n], (into, n), (from_here, n)

        held = [total[0]] + [swap_slot(total[j], j, group) for j in range(1, group)]

        block = block_sum(held)
        parts = local_parts(data, block)
        keys, rests = block[0], block[1]
        carry = jnp.zeros_like(block)
        bit = 2 * group
        while bit < count:
            upper = (index & bit) != 0
            if 2 * bit < count:
                got = swap(jnp.stack([keys, rests]), bit)
                keys, rests = keys + got[0], rests + got[1]
                got_keys, got_rests = got[0], got[1]
            else:
                got_keys = got_rests = swap(jnp.where(upper, rests, keys), bit)
            carry = carry + jnp.stack(
                [jnp.where(upper, got_keys, 0.0), jnp.where(upper, 0.0, got_rests)]
            )
            bit *= 2

        around = [outside_of(carry, held, j, parts[0]) for j in range(group)]
        around = [swap_slot(x, j, group) if j else x for j, x in enumerate(around)]
        soon, late = (0, group - 1), tuple(range(group - 2, 0, -1))
        mine, theirs = shares_of(inner, outer, around, soon)
        other = swap(theirs, 1)
        *done, mark = final_sums(data, parts, [mine], [(False, soon)])
        late_mine, late_theirs = shares_of(inner, outer, around, late, [mark])
        late_other = swap(late_theirs, 1)
        pieces = [(True, soon), (False, late)]
        done = final_sums(data, parts, [other, late_mine], pieces, done)
        return tuple(final_sums(data, parts, [late_other], [(True, late)], done))

    return body


def solution(mesh):
    count = mesh.shape["seq"]

    def run(queries, key_rows, value_rows, grad_out):
        heads = queries.shape[0] // mesh.shape["head"]
        tokens = queries.shape[1] // count
        group = heads // 2
        powers = all(n > 0 and n & (n - 1) == 0 for n in (count, group))
        fits = powers and heads == 2 * group and group >= 4 and tokens == TILE and count >= 4 * group
        body = sliced_body(group) if fits else plain_body
        return jax.shard_map(
            body, mesh=mesh, in_specs=(SPEC,) * 4, out_specs=(SPEC,) * 3, check_vma=False
        )(queries, key_rows, value_rows, grad_out)

    return run
```

```python
import functools

import jax
import jax.numpy as jnp
from jax import lax
from jax.experimental import pallas as pl
from jax.experimental.pallas import tpu as pltpu
from jax.sharding import PartitionSpec as P

TILE = 256
SPEC = P("head", "seq", None)
F32 = jnp.float32
BF16 = jnp.bfloat16


def entering(x, axis, combine, identity, reverse):
    count, place = (lax.axis_size(axis), lax.axis_index(axis))
    everything = lax.all_gather(x, axis)
    start = jnp.broadcast_to(jnp.asarray(identity, x.dtype), x.shape)

    def turn(k, before):
        at = count - 1 - k if reverse else k
        reached = at > place if reverse else at < place
        new = combine(before, everything[at])
        return jnp.where(reached, new, before)

    return lax.fori_loop(0, count, turn, start)


def add_states(earlier, latter):
    return earlier + latter


def plain_body(queries, key_rows, value_rows, grad_out):
    head_count, tokens, head_width = queries.shape
    tile_count = tokens // TILE
    tile_shape = (head_count, tile_count, TILE, head_width)
    query_tiles = queries.reshape(tile_shape)
    key_tiles = key_rows.reshape(tile_shape)
    value_tiles = value_rows.reshape(tile_shape)
    grad_tiles = grad_out.reshape(tile_shape)

    def product(rule, a, b):
        return jnp.einsum(rule, a, b, preferred_element_type=F32)

    key_state = product("hjsa,hjsb->hjab", key_tiles, value_tiles)
    query_state = product("hjta,hjtb->hjab", query_tiles, grad_tiles)
    local_keys = jnp.sum(key_state, 1)
    local_queries = jnp.sum(query_state, 1)
    blank_state = jnp.zeros_like(local_keys)
    incoming = entering(local_keys, "seq", add_states, blank_state, False)
    outgoing = entering(local_queries, "seq", add_states, blank_state, True)
    zero_state = jnp.zeros((head_count, 1, head_width, head_width), F32)
    earlier_states = incoming[:, None] + jnp.concatenate(
        [zero_state, jnp.cumsum(key_state, 1)[:, :-1]], 1
    )
    later_states = outgoing[:, None] + jnp.concatenate(
        [jnp.cumsum(query_state[:, ::-1], 1)[:, ::-1][:, 1:], zero_state], 1
    )
    earlier_states = earlier_states.astype(BF16)
    later_states = later_states.astype(BF16)
    causal = (jnp.arange(TILE)[:, None] >= jnp.arange(TILE)[None, :])[None, None]
    out_scores = product("hjta,hjsa->hjts", grad_tiles, value_tiles)
    out_scores = jnp.where(causal, out_scores, 0.0).astype(BF16)
    attn_scores = product("hjta,hjsa->hjts", query_tiles, key_tiles)
    attn_scores = jnp.where(causal, attn_scores, 0.0).astype(BF16)
    grad_query = product("hjts,hjsa->hjta", out_scores, key_tiles)
    grad_query = grad_query + product("hjtb,hjab->hjta", grad_tiles, earlier_states)
    grad_key = product("hjts,hjta->hjsa", out_scores, query_tiles)
    grad_key = grad_key + product("hjsb,hjab->hjsa", value_tiles, later_states)
    grad_value = product("hjts,hjtb->hjsb", attn_scores, grad_tiles)
    grad_value = grad_value + product("hjsa,hjab->hjsb", key_tiles, later_states)
    flat_shape = (head_count, tokens, head_width)
    return tuple(
        x.astype(BF16).reshape(flat_shape) for x in (grad_query, grad_key, grad_value)
    )


WHOLE = pl.BlockSpec(memory_space=pltpu.VMEM)
PLACED = pl.BlockSpec(memory_space=pl.ANY)
FAR = pl.BlockSpec(memory_space=pltpu.HBM)
ROOM = pltpu.CompilerParams(vmem_limit_bytes=16 * 2**20)


def near(x):
    return pltpu.with_memory_space_constraint(x, pltpu.VMEM)


def far(x):
    return pltpu.with_memory_space_constraint(x, pltpu.HBM)


def dot(a, b, da, db):
    return lax.dot_general(a, b, (((da,), (db,)), ((), ())), preferred_element_type=F32)


def turned(slot, group):
    return (group - slot) & (group - 1)


def place_of(group):
    index = lax.axis_index("seq")
    return index & 1, (index >> 1) & (group - 1)


def partner(core, rank, slot, group):
    return rank ^ (slot + core * (turned(slot, group) - slot))


def away_kernel(q, k, v, g, out, qs, ks, vs, gs, sems, *, part):
    slots = q.shape[0] // 2
    core, rank = place_of(slots)
    core = 1 - core
    copies = []
    for n, (there, here) in enumerate(((k, ks), (v, vs), (q, qs), (g, gs))):
        for m, slot in enumerate(part):
            head = core * slots + partner(core, rank, slot, slots)
            copies.append(pltpu.make_async_copy(there.at[head], here.at[m], sems.at[n, m]))
            copies[-1].start()
    for copy in copies[: 2 * len(part)]:
        copy.wait()
    for m in range(len(part)):
        out[m, 0] = dot(ks[m], vs[m], 0, 0)
    for copy in copies[2 * len(part) :]:
        copy.wait()
    for m in range(len(part)):
        out[m, 1] = dot(qs[m], gs[m], 0, 0)


def near_kernel(q, k, v, g, *outs, parts, other):
    slots = q.shape[0] // 2
    core, rank = place_of(slots)
    core = 1 - core if other else core
    for out, part in zip(outs, parts):
        for m, slot in enumerate(part):
            head = core * slots + partner(core, rank, slot, slots)
            out[m, 0] = dot(k[head], v[head], 0, 0)
            out[m, 1] = dot(q[head], g[head], 0, 0)


def state_call(kernel, data, parts, place, spec, scratch):
    _, tokens, width = data[0].shape
    count = sum(len(part) for part in parts)
    return pl.pallas_call(
        kernel,
        out_shape=[pltpu.VMEM((len(part), 2, width, width), F32) for part in parts],
        in_specs=[spec] * 4,
        out_specs=[WHOLE] * len(parts),
        scratch_shapes=scratch,
        compiler_params=ROOM,
        cost_estimate=pl.CostEstimate(
            flops=count * 4 * tokens * width * width,
            bytes_accessed=count * 8 * tokens * width,
            transcendentals=0,
        ),
    )(*[place(x) for x in data])


def away_states(data, part):
    _, tokens, width = data[0].shape
    scratch = [pltpu.VMEM((len(part), tokens, width), BF16)] * 4
    scratch.append(pltpu.SemaphoreType.DMA((4, len(part))))
    kernel = functools.partial(away_kernel, part=part)
    return state_call(kernel, data, [part], far, FAR, scratch)


def near_states(data, parts, other):
    kernel = functools.partial(near_kernel, parts=parts, other=other)
    return state_call(kernel, data, parts, near, WHOLE, [])


def total_kernel(came, keep, *refs):
    *totals, inner, outer = refs
    core = lax.axis_index("seq") & 1
    for i, out in enumerate(totals):
        out[...] = came[i] + keep[i]
        inner[i] = jnp.where(core == 0, came[i, 1], came[i, 0])
        outer[i] = jnp.where(core == 0, keep[i, 0], keep[i, 1])


def totals_of(came, keep):
    slots, _, width, _ = keep.shape
    return pl.pallas_call(
        total_kernel,
        out_shape=[pltpu.VMEM((2, width, width), F32)] * slots
        + [pltpu.VMEM((slots, width, width), F32)] * 2,
        in_specs=[WHOLE] * 2,
        out_specs=[WHOLE] * (slots + 2),
        compiler_params=ROOM,
    )(near(came), near(keep))


def outside_kernel(after, carry, *refs, slot, group):
    out = refs[-1]
    core, rank = place_of(group)
    earlier, later = carry[0], carry[1]
    there = partner(core, rank, slot, group)
    for i in range(group):
        if i != slot:
            before = partner(core, rank, i, group) < there
            earlier = earlier + jnp.where(before, refs[i][0], 0.0)
            later = later + jnp.where(before, 0.0, refs[i][1])
    out[0] = earlier
    out[1] = later


def outside_of(carry, held, slot, after):
    return pl.pallas_call(
        functools.partial(outside_kernel, slot=slot, group=len(held)),
        out_shape=pltpu.VMEM(carry.shape, F32),
        in_specs=[PLACED] + [WHOLE] * (1 + len(held)),
        out_specs=WHOLE,
        compiler_params=ROOM,
    )(near(after), near(carry), *[near(x) for x in held])


def share_kernel(*refs, rows):
    mine, theirs = refs[-2:]
    first = lax.axis_index("seq") & 1 == 0
    for n, i in enumerate(rows):
        inner, outer, around = refs[3 * n : 3 * n + 3]
        earlier, later = around[0], around[1]
        mine[n, 0] = earlier + jnp.where(first, 0.0, inner[i])
        mine[n, 1] = later + jnp.where(first, inner[i], 0.0)
        theirs[n, 0] = earlier + jnp.where(first, outer[i], 0.0)
        theirs[n, 1] = later + jnp.where(first, 0.0, outer[i])


def shares_of(inner, outer, around, slots, after=()):
    shape = (len(slots), *around[0].shape)
    given = [x for i in slots for x in (inner[i][0], outer[i][0], around[i])]
    return pl.pallas_call(
        functools.partial(share_kernel, rows=[inner[i][1] for i in slots]),
        out_shape=[pltpu.VMEM(shape, F32)] * 2,
        in_specs=[WHOLE] * len(given) + [PLACED] * len(after),
        out_specs=[WHOLE] * 2,
        compiler_params=ROOM,
    )(*[near(x) for x in (*given, *after)])


def local_kernel(qs, ks, vs, gs, after, gq, gk, gv):
    heads, tokens, _ = qs.shape
    row = lax.broadcasted_iota(jnp.int32, (tokens, tokens), 0)
    col = lax.broadcasted_iota(jnp.int32, (tokens, tokens), 1)
    for i in range(heads):
        q, k, v, g = qs[i], ks[i], vs[i], gs[i]
        score = jnp.where(row >= col, dot(g, v, 1, 1), 0.0).astype(BF16)
        gq[i] = dot(score, k, 1, 0)
        score = jnp.where(row <= col, dot(v, g, 1, 1), 0.0).astype(BF16)
        gk[i] = dot(score, q, 1, 0)
        score = jnp.where(row <= col, dot(k, q, 1, 1), 0.0).astype(BF16)
        gv[i] = dot(score, g, 1, 0)


def local_parts(data, after):
    heads, tokens, width = data[0].shape
    return pl.pallas_call(
        local_kernel,
        out_shape=[pltpu.VMEM(data[0].shape, F32)] * 3,
        in_specs=[WHOLE] * 4 + [PLACED],
        out_specs=[WHOLE] * 3,
        compiler_params=ROOM,
        cost_estimate=pl.CostEstimate(
            flops=heads * 12 * tokens * tokens * width,
            bytes_accessed=heads * 20 * tokens * width,
            transcendentals=0,
        ),
    )(*[near(x) for x in data], near(after))


def block_kernel(*refs):
    out = refs[-1]
    total = refs[0][...]
    for x in refs[1:-1]:
        total = total + x[...]
    out[...] = total


def block_sum(held):
    return pl.pallas_call(
        block_kernel,
        out_shape=pltpu.VMEM(held[0].shape, F32),
        in_specs=[WHOLE] * len(held),
        out_specs=WHOLE,
        compiler_params=ROOM,
    )(*[near(x) for x in held])


def final_kernel(k, v, g, lq, lk, lv, *refs, pieces, given):
    bq, bk, bv, sems = refs[-4:]
    gq, gk, gv, *marks = refs[len(pieces) + given : -4]
    for mark in marks:
        mark[...] = jnp.zeros_like(mark)
    half = k.shape[0] // 2
    core, rank = place_of(half)
    copies = []
    for state, (other, slots) in zip(refs, pieces):
        side = 1 - core if other else core
        for i, slot in enumerate(slots):
            earlier, later = state[i, 0].astype(BF16), state[i, 1].astype(BF16)
            head, n = side * half + partner(side, rank, slot, half), len(copies) // 3
            bq[n] = (lq[head] + dot(g[head], earlier, 1, 1)).astype(BF16)
            bk[n] = (lk[head] + dot(v[head], later, 1, 1)).astype(BF16)
            bv[n] = (lv[head] + dot(k[head], later, 1, 0)).astype(BF16)
            for m, (here, there) in enumerate(((bq, gq), (bk, gk), (bv, gv))):
                copies.append(pltpu.make_async_copy(here.at[n], there.at[head], sems.at[n, m]))
                copies[-1].start()
    for copy in copies:
        copy.wait()


def final_sums(data, parts, states, pieces, filled=()):
    _, tokens, width = data[0].shape
    count = sum(len(slots) for _, slots in pieces)
    held = 6 + len(states)
    return pl.pallas_call(
        functools.partial(final_kernel, pieces=pieces, given=len(filled)),
        out_shape=[jax.ShapeDtypeStruct(data[0].shape, BF16)] * 3
        + [pltpu.VMEM((8, width), F32)] * (not filled),
        in_specs=[WHOLE] * held + [PLACED] * len(filled),
        out_specs=[PLACED] * 3 + [WHOLE] * (not filled),
        input_output_aliases={held + n: n for n in range(len(filled))},
        scratch_shapes=[pltpu.VMEM((count, tokens, width), BF16)] * 3
        + [pltpu.SemaphoreType.DMA((count, 3))],
        compiler_params=ROOM,
        cost_estimate=pl.CostEstimate(
            flops=count * 6 * tokens * width * width,
            bytes_accessed=count * 6 * tokens * width,
            transcendentals=0,
        ),
    )(*[near(x) for x in (*data[1:], *parts, *states)], *filled)


def swap(x, mask):
    count = lax.axis_size("seq")
    return lax.ppermute(x, "seq", [(i, i ^ mask) for i in range(count)])


def swap_slot(x, slot, group):
    count = lax.axis_size("seq")
    masks = (2 * slot, 2 * turned(slot, group))
    return lax.ppermute(x, "seq", [(i, i ^ masks[i & 1]) for i in range(count)])


def sliced_body(group):
    def body(queries, key_rows, value_rows, grad_out):
        count, index = lax.axis_size("seq"), lax.axis_index("seq")
        slots = group
        data = (queries, key_rows, value_rows, grad_out)

        split = ((1, 2), (0, *range(3, slots)))
        away = away_states(data, split[0]) + near_states(data, split[1:], True)
        keep = near_states(data, split, False)
        came = [swap(x, 1) for x in away]
        total, inner, outer = {}, {}, {}
        for part, a, b in zip(split, came, keep):
            *sums, into, from_here = totals_of(a, b)
            for n, j in enumerate(part):
                total[j], inner[j], outer[j] = sums[n], (into, n), (from_here, n)

        held = [total[0]] + [swap_slot(total[j], j, group) for j in range(1, group)]

        block = block_sum(held)
        parts = local_parts(data, block)
        keys, rests = block[0], block[1]
        carry = jnp.zeros_like(block)
        bit = 2 * group
        while bit < count:
            upper = (index & bit) != 0
            if 2 * bit < count:
                got = swap(jnp.stack([keys, rests]), bit)
                keys, rests = keys + got[0], rests + got[1]
                got_keys, got_rests = got[0], got[1]
            else:
                got_keys = got_rests = swap(jnp.where(upper, rests, keys), bit)
            carry = carry + jnp.stack(
                [jnp.where(upper, got_keys, 0.0), jnp.where(upper, 0.0, got_rests)]
            )
            bit *= 2

        around = [outside_of(carry, held, j, parts[0]) for j in range(group)]
        around = [swap_slot(x, j, group) if j else x for j, x in enumerate(around)]
        soon, late = (0, group - 1), tuple(range(group - 2, 0, -1))
        mine, theirs = shares_of(inner, outer, around, soon)
        other = swap(theirs, 1)
        *done, mark = final_sums(data, parts, [mine], [(False, soon)])
        late_mine, late_theirs = shares_of(inner, outer, around, late, [mark])
        late_other = swap(late_theirs, 1)
        pieces = [(True, soon), (False, late)]
        done = final_sums(data, parts, [other, late_mine], pieces, done)
        return tuple(final_sums(data, parts, [late_other], [(True, late)], done))

    return body


def solution(mesh):
    count = mesh.shape["seq"]

    def run(queries, key_rows, value_rows, grad_out):
        heads = queries.shape[0] // mesh.shape["head"]
        tokens = queries.shape[1] // count
        group = heads // 2
        powers = all(n > 0 and n & (n - 1) == 0 for n in (count, group))
        fits = powers and heads == 2 * group and group >= 4 and tokens == TILE and count >= 4 * group
        body = sliced_body(group) if fits else plain_body
        return jax.shard_map(
            body, mesh=mesh, in_specs=(SPEC,) * 4, out_specs=(SPEC,) * 3, check_vma=False
        )(queries, key_rows, value_rows, grad_out)

    return run
```

```python
import functools

import jax
import jax.numpy as jnp
from jax import lax
from jax.experimental import pallas as pl
from jax.experimental.pallas import tpu as pltpu
from jax.sharding import PartitionSpec as P

TILE = 256
SPEC = P("head", "seq", None)
F32 = jnp.float32
BF16 = jnp.bfloat16


def entering(x, axis, combine, identity, reverse):
    count, place = (lax.axis_size(axis), lax.axis_index(axis))
    everything = lax.all_gather(x, axis)
    start = jnp.broadcast_to(jnp.asarray(identity, x.dtype), x.shape)

    def turn(k, before):
        at = count - 1 - k if reverse else k
        reached = at > place if reverse else at < place
        new = combine(before, everything[at])
        return jnp.where(reached, new, before)

    return lax.fori_loop(0, count, turn, start)


def add_states(earlier, latter):
    return earlier + latter


def plain_body(queries, key_rows, value_rows, grad_out):
    head_count, tokens, head_width = queries.shape
    tile_count = tokens // TILE
    tile_shape = (head_count, tile_count, TILE, head_width)
    query_tiles = queries.reshape(tile_shape)
    key_tiles = key_rows.reshape(tile_shape)
    value_tiles = value_rows.reshape(tile_shape)
    grad_tiles = grad_out.reshape(tile_shape)

    def product(rule, a, b):
        return jnp.einsum(rule, a, b, preferred_element_type=F32)

    key_state = product("hjsa,hjsb->hjab", key_tiles, value_tiles)
    query_state = product("hjta,hjtb->hjab", query_tiles, grad_tiles)
    local_keys = jnp.sum(key_state, 1)
    local_queries = jnp.sum(query_state, 1)
    blank_state = jnp.zeros_like(local_keys)
    incoming = entering(local_keys, "seq", add_states, blank_state, False)
    outgoing = entering(local_queries, "seq", add_states, blank_state, True)
    zero_state = jnp.zeros((head_count, 1, head_width, head_width), F32)
    earlier_states = incoming[:, None] + jnp.concatenate(
        [zero_state, jnp.cumsum(key_state, 1)[:, :-1]], 1
    )
    later_states = outgoing[:, None] + jnp.concatenate(
        [jnp.cumsum(query_state[:, ::-1], 1)[:, ::-1][:, 1:], zero_state], 1
    )
    earlier_states = earlier_states.astype(BF16)
    later_states = later_states.astype(BF16)
    causal = (jnp.arange(TILE)[:, None] >= jnp.arange(TILE)[None, :])[None, None]
    out_scores = product("hjta,hjsa->hjts", grad_tiles, value_tiles)
    out_scores = jnp.where(causal, out_scores, 0.0).astype(BF16)
    attn_scores = product("hjta,hjsa->hjts", query_tiles, key_tiles)
    attn_scores = jnp.where(causal, attn_scores, 0.0).astype(BF16)
    grad_query = product("hjts,hjsa->hjta", out_scores, key_tiles)
    grad_query = grad_query + product("hjtb,hjab->hjta", grad_tiles, earlier_states)
    grad_key = product("hjts,hjta->hjsa", out_scores, query_tiles)
    grad_key = grad_key + product("hjsb,hjab->hjsa", value_tiles, later_states)
    grad_value = product("hjts,hjtb->hjsb", attn_scores, grad_tiles)
    grad_value = grad_value + product("hjsa,hjab->hjsb", key_tiles, later_states)
    flat_shape = (head_count, tokens, head_width)
    return tuple(
        x.astype(BF16).reshape(flat_shape) for x in (grad_query, grad_key, grad_value)
    )


WHOLE = pl.BlockSpec(memory_space=pltpu.VMEM)
PLACED = pl.BlockSpec(memory_space=pl.ANY)
FAR = pl.BlockSpec(memory_space=pltpu.HBM)
ROOM = pltpu.CompilerParams(vmem_limit_bytes=16 * 2**20)


def near(x):
    return pltpu.with_memory_space_constraint(x, pltpu.VMEM)


def far(x):
    return pltpu.with_memory_space_constraint(x, pltpu.HBM)


def dot(a, b, da, db):
    return lax.dot_general(a, b, (((da,), (db,)), ((), ())), preferred_element_type=F32)


def turned(slot, group):
    return (group - slot) & (group - 1)


def place_of(group):
    index = lax.axis_index("seq")
    return index & 1, (index >> 1) & (group - 1)


def partner(core, rank, slot, group):
    return rank ^ (slot + core * (turned(slot, group) - slot))


def away_kernel(q, k, v, g, out, qs, ks, vs, gs, sems, *, part):
    slots = q.shape[0] // 2
    core, rank = place_of(slots)
    core = 1 - core
    copies = []
    for n, (there, here) in enumerate(((k, ks), (v, vs), (q, qs), (g, gs))):
        for m, slot in enumerate(part):
            head = core * slots + partner(core, rank, slot, slots)
            copies.append(pltpu.make_async_copy(there.at[head], here.at[m], sems.at[n, m]))
            copies[-1].start()
    for copy in copies:
        copy.wait()
    for m in range(len(part)):
        out[m, 0] = dot(ks[m], vs[m], 0, 0)
        out[m, 1] = dot(qs[m], gs[m], 0, 0)


def near_kernel(q, k, v, g, *outs, parts, other):
    slots = q.shape[0] // 2
    core, rank = place_of(slots)
    core = 1 - core if other else core
    for out, part in zip(outs, parts):
        for m, slot in enumerate(part):
            head = core * slots + partner(core, rank, slot, slots)
            out[m, 0] = dot(k[head], v[head], 0, 0)
            out[m, 1] = dot(q[head], g[head], 0, 0)


def state_call(kernel, data, parts, place, spec, scratch):
    _, tokens, width = data[0].shape
    count = sum(len(part) for part in parts)
    return pl.pallas_call(
        kernel,
        out_shape=[pltpu.VMEM((len(part), 2, width, width), F32) for part in parts],
        in_specs=[spec] * 4,
        out_specs=[WHOLE] * len(parts),
        scratch_shapes=scratch,
        compiler_params=ROOM,
        cost_estimate=pl.CostEstimate(
            flops=count * 4 * tokens * width * width,
            bytes_accessed=count * 8 * tokens * width,
            transcendentals=0,
        ),
    )(*[place(x) for x in data])


def away_states(data, part):
    _, tokens, width = data[0].shape
    scratch = [pltpu.VMEM((len(part), tokens, width), BF16)] * 4
    scratch.append(pltpu.SemaphoreType.DMA((4, len(part))))
    kernel = functools.partial(away_kernel, part=part)
    return state_call(kernel, data, [part], far, FAR, scratch)


def near_states(data, parts, other):
    kernel = functools.partial(near_kernel, parts=parts, other=other)
    return state_call(kernel, data, parts, near, WHOLE, [])


def total_kernel(came, keep, *refs):
    *totals, inner, outer = refs
    core = lax.axis_index("seq") & 1
    for i, out in enumerate(totals):
        out[...] = came[i] + keep[i]
        inner[i] = jnp.where(core == 0, came[i, 1], came[i, 0])
        outer[i] = jnp.where(core == 0, keep[i, 0], keep[i, 1])


def totals_of(came, keep):
    slots, _, width, _ = keep.shape
    return pl.pallas_call(
        total_kernel,
        out_shape=[pltpu.VMEM((2, width, width), F32)] * slots
        + [pltpu.VMEM((slots, width, width), F32)] * 2,
        in_specs=[WHOLE] * 2,
        out_specs=[WHOLE] * (slots + 2),
        compiler_params=ROOM,
    )(near(came), near(keep))


def outside_kernel(carry, *refs, slot, group):
    out = refs[-1]
    core, rank = place_of(group)
    earlier, later = carry[0], carry[1]
    there = partner(core, rank, slot, group)
    for i in range(group):
        if i != slot:
            before = partner(core, rank, i, group) < there
            earlier = earlier + jnp.where(before, refs[i][0], 0.0)
            later = later + jnp.where(before, 0.0, refs[i][1])
    out[0] = earlier
    out[1] = later


def outside_of(carry, held, slot):
    return pl.pallas_call(
        functools.partial(outside_kernel, slot=slot, group=len(held)),
        out_shape=pltpu.VMEM(carry.shape, F32),
        in_specs=[WHOLE] * (1 + len(held)),
        out_specs=WHOLE,
        compiler_params=ROOM,
    )(near(carry), *[near(x) for x in held])


def share_kernel(*refs, rows):
    mine, theirs = refs[-2:]
    first = lax.axis_index("seq") & 1 == 0
    for n, i in enumerate(rows):
        inner, outer, around = refs[3 * n : 3 * n + 3]
        earlier, later = around[0], around[1]
        mine[n, 0] = earlier + jnp.where(first, 0.0, inner[i])
        mine[n, 1] = later + jnp.where(first, inner[i], 0.0)
        theirs[n, 0] = earlier + jnp.where(first, outer[i], 0.0)
        theirs[n, 1] = later + jnp.where(first, 0.0, outer[i])


def shares_of(inner, outer, around, slots, after=()):
    shape = (len(slots), *around[0].shape)
    given = [x for i in slots for x in (inner[i][0], outer[i][0], around[i])]
    return pl.pallas_call(
        functools.partial(share_kernel, rows=[inner[i][1] for i in slots]),
        out_shape=[pltpu.VMEM(shape, F32)] * 2,
        in_specs=[WHOLE] * len(given) + [PLACED] * len(after),
        out_specs=[WHOLE] * 2,
        compiler_params=ROOM,
    )(*[near(x) for x in (*given, *after)])


def local_kernel(qs, ks, vs, gs, after, gq, gk, gv):
    heads, tokens, _ = qs.shape
    row = lax.broadcasted_iota(jnp.int32, (tokens, tokens), 0)
    col = lax.broadcasted_iota(jnp.int32, (tokens, tokens), 1)
    for i in range(heads):
        q, k, v, g = qs[i], ks[i], vs[i], gs[i]
        score = jnp.where(row >= col, dot(g, v, 1, 1), 0.0).astype(BF16)
        gq[i] = dot(score, k, 1, 0)
        score = jnp.where(row <= col, dot(v, g, 1, 1), 0.0).astype(BF16)
        gk[i] = dot(score, q, 1, 0)
        score = jnp.where(row <= col, dot(k, q, 1, 1), 0.0).astype(BF16)
        gv[i] = dot(score, g, 1, 0)


def local_parts(data, after):
    heads, tokens, width = data[0].shape
    return pl.pallas_call(
        local_kernel,
        out_shape=[pltpu.VMEM(data[0].shape, F32)] * 3,
        in_specs=[WHOLE] * 4 + [PLACED],
        out_specs=[WHOLE] * 3,
        compiler_params=ROOM,
        cost_estimate=pl.CostEstimate(
            flops=heads * 12 * tokens * tokens * width,
            bytes_accessed=heads * 20 * tokens * width,
            transcendentals=0,
        ),
    )(*[near(x) for x in data], near(after))


def block_kernel(after, *refs):
    out = refs[-1]
    total = refs[0][...]
    for x in refs[1:-1]:
        total = total + x[...]
    out[...] = total


def block_sum(held, after):
    return pl.pallas_call(
        block_kernel,
        out_shape=pltpu.VMEM(held[0].shape, F32),
        in_specs=[PLACED] + [WHOLE] * len(held),
        out_specs=WHOLE,
        compiler_params=ROOM,
    )(near(after), *[near(x) for x in held])


def final_kernel(k, v, g, lq, lk, lv, *refs, pieces, given):
    bq, bk, bv, sems = refs[-4:]
    gq, gk, gv, *marks = refs[len(pieces) + given : -4]
    for mark in marks:
        mark[...] = jnp.zeros_like(mark)
    half = k.shape[0] // 2
    core, rank = place_of(half)
    copies = []
    for state, (other, slots) in zip(refs, pieces):
        side = 1 - core if other else core
        for i, slot in enumerate(slots):
            earlier, later = state[i, 0].astype(BF16), state[i, 1].astype(BF16)
            head, n = side * half + partner(side, rank, slot, half), len(copies) // 3
            bq[n] = (lq[head] + dot(g[head], earlier, 1, 1)).astype(BF16)
            bk[n] = (lk[head] + dot(v[head], later, 1, 1)).astype(BF16)
            bv[n] = (lv[head] + dot(k[head], later, 1, 0)).astype(BF16)
            for m, (here, there) in enumerate(((bq, gq), (bk, gk), (bv, gv))):
                copies.append(pltpu.make_async_copy(here.at[n], there.at[head], sems.at[n, m]))
                copies[-1].start()
    for copy in copies:
        copy.wait()


def final_sums(data, parts, states, pieces, filled=()):
    _, tokens, width = data[0].shape
    count = sum(len(slots) for _, slots in pieces)
    held = 6 + len(states)
    return pl.pallas_call(
        functools.partial(final_kernel, pieces=pieces, given=len(filled)),
        out_shape=[jax.ShapeDtypeStruct(data[0].shape, BF16)] * 3
        + [pltpu.VMEM((8, width), F32)] * (not filled),
        in_specs=[WHOLE] * held + [PLACED] * len(filled),
        out_specs=[PLACED] * 3 + [WHOLE] * (not filled),
        input_output_aliases={held + n: n for n in range(len(filled))},
        scratch_shapes=[pltpu.VMEM((count, tokens, width), BF16)] * 3
        + [pltpu.SemaphoreType.DMA((count, 3))],
        compiler_params=ROOM,
        cost_estimate=pl.CostEstimate(
            flops=count * 6 * tokens * width * width,
            bytes_accessed=count * 6 * tokens * width,
            transcendentals=0,
        ),
    )(*[near(x) for x in (*data[1:], *parts, *states)], *filled)


def swap(x, mask):
    count = lax.axis_size("seq")
    return lax.ppermute(x, "seq", [(i, i ^ mask) for i in range(count)])


def swap_slot(x, slot, group):
    count = lax.axis_size("seq")
    masks = (2 * slot, 2 * turned(slot, group))
    return lax.ppermute(x, "seq", [(i, i ^ masks[i & 1]) for i in range(count)])


def sliced_body(group):
    def body(queries, key_rows, value_rows, grad_out):
        count, index = lax.axis_size("seq"), lax.axis_index("seq")
        slots = group
        data = (queries, key_rows, value_rows, grad_out)

        split = ((1, 2), (0, *range(3, slots)))
        away = away_states(data, split[0]) + near_states(data, split[1:], True)
        keep = near_states(data, split, False)
        came = [swap(x, 1) for x in away]
        total, inner, outer = {}, {}, {}
        for part, a, b in zip(split, came, keep):
            *sums, into, from_here = totals_of(a, b)
            for n, j in enumerate(part):
                total[j], inner[j], outer[j] = sums[n], (into, n), (from_here, n)

        held = [total[0]] + [swap_slot(total[j], j, group) for j in range(1, group)]
        parts = local_parts(data, total[0])

        block = block_sum(held, parts[0])
        keys, rests = block[0], block[1]
        carry = jnp.zeros_like(block)
        bit = 2 * group
        while bit < count:
            upper = (index & bit) != 0
            if 2 * bit < count:
                got = swap(jnp.stack([keys, rests]), bit)
                keys, rests = keys + got[0], rests + got[1]
                got_keys, got_rests = got[0], got[1]
            else:
                got_keys = got_rests = swap(jnp.where(upper, rests, keys), bit)
            carry = carry + jnp.stack(
                [jnp.where(upper, got_keys, 0.0), jnp.where(upper, 0.0, got_rests)]
            )
            bit *= 2

        around = [outside_of(carry, held, j) for j in range(group)]
        around = [swap_slot(x, j, group) if j else x for j, x in enumerate(around)]
        soon, late = (0, group - 1), tuple(range(group - 2, 0, -1))
        mine, theirs = shares_of(inner, outer, around, soon)
        other = swap(theirs, 1)
        *done, mark = final_sums(data, parts, [mine], [(False, soon)])
        late_mine, late_theirs = shares_of(inner, outer, around, late, [mark])
        late_other = swap(late_theirs, 1)
        pieces = [(True, soon), (False, late)]
        done = final_sums(data, parts, [other, late_mine], pieces, done)
        return tuple(final_sums(data, parts, [late_other], [(True, late)], done))

    return body


def solution(mesh):
    count = mesh.shape["seq"]

    def run(queries, key_rows, value_rows, grad_out):
        heads = queries.shape[0] // mesh.shape["head"]
        tokens = queries.shape[1] // count
        group = heads // 2
        powers = all(n > 0 and n & (n - 1) == 0 for n in (count, group))
        fits = powers and heads == 2 * group and group >= 4 and tokens == TILE and count >= 4 * group
        body = sliced_body(group) if fits else plain_body
        return jax.shard_map(
            body, mesh=mesh, in_specs=(SPEC,) * 4, out_specs=(SPEC,) * 3, check_vma=False
        )(queries, key_rows, value_rows, grad_out)

    return run
```

```python
import functools

import jax
import jax.numpy as jnp
from jax import lax
from jax.experimental import pallas as pl
from jax.experimental.pallas import tpu as pltpu
from jax.sharding import PartitionSpec as P

TILE = 256
SPEC = P("head", "seq", None)
F32 = jnp.float32
BF16 = jnp.bfloat16


def entering(x, axis, combine, identity, reverse):
    count, place = (lax.axis_size(axis), lax.axis_index(axis))
    everything = lax.all_gather(x, axis)
    start = jnp.broadcast_to(jnp.asarray(identity, x.dtype), x.shape)

    def turn(k, before):
        at = count - 1 - k if reverse else k
        reached = at > place if reverse else at < place
        new = combine(before, everything[at])
        return jnp.where(reached, new, before)

    return lax.fori_loop(0, count, turn, start)


def add_states(earlier, latter):
    return earlier + latter


def plain_body(queries, key_rows, value_rows, grad_out):
    head_count, tokens, head_width = queries.shape
    tile_count = tokens // TILE
    tile_shape = (head_count, tile_count, TILE, head_width)
    query_tiles = queries.reshape(tile_shape)
    key_tiles = key_rows.reshape(tile_shape)
    value_tiles = value_rows.reshape(tile_shape)
    grad_tiles = grad_out.reshape(tile_shape)

    def product(rule, a, b):
        return jnp.einsum(rule, a, b, preferred_element_type=F32)

    key_state = product("hjsa,hjsb->hjab", key_tiles, value_tiles)
    query_state = product("hjta,hjtb->hjab", query_tiles, grad_tiles)
    local_keys = jnp.sum(key_state, 1)
    local_queries = jnp.sum(query_state, 1)
    blank_state = jnp.zeros_like(local_keys)
    incoming = entering(local_keys, "seq", add_states, blank_state, False)
    outgoing = entering(local_queries, "seq", add_states, blank_state, True)
    zero_state = jnp.zeros((head_count, 1, head_width, head_width), F32)
    earlier_states = incoming[:, None] + jnp.concatenate(
        [zero_state, jnp.cumsum(key_state, 1)[:, :-1]], 1
    )
    later_states = outgoing[:, None] + jnp.concatenate(
        [jnp.cumsum(query_state[:, ::-1], 1)[:, ::-1][:, 1:], zero_state], 1
    )
    earlier_states = earlier_states.astype(BF16)
    later_states = later_states.astype(BF16)
    causal = (jnp.arange(TILE)[:, None] >= jnp.arange(TILE)[None, :])[None, None]
    out_scores = product("hjta,hjsa->hjts", grad_tiles, value_tiles)
    out_scores = jnp.where(causal, out_scores, 0.0).astype(BF16)
    attn_scores = product("hjta,hjsa->hjts", query_tiles, key_tiles)
    attn_scores = jnp.where(causal, attn_scores, 0.0).astype(BF16)
    grad_query = product("hjts,hjsa->hjta", out_scores, key_tiles)
    grad_query = grad_query + product("hjtb,hjab->hjta", grad_tiles, earlier_states)
    grad_key = product("hjts,hjta->hjsa", out_scores, query_tiles)
    grad_key = grad_key + product("hjsb,hjab->hjsa", value_tiles, later_states)
    grad_value = product("hjts,hjtb->hjsb", attn_scores, grad_tiles)
    grad_value = grad_value + product("hjsa,hjab->hjsb", key_tiles, later_states)
    flat_shape = (head_count, tokens, head_width)
    return tuple(
        x.astype(BF16).reshape(flat_shape) for x in (grad_query, grad_key, grad_value)
    )


WHOLE = pl.BlockSpec(memory_space=pltpu.VMEM)
PLACED = pl.BlockSpec(memory_space=pl.ANY)
FAR = pl.BlockSpec(memory_space=pltpu.HBM)
ROOM = pltpu.CompilerParams(vmem_limit_bytes=16 * 2**20)


def near(x):
    return pltpu.with_memory_space_constraint(x, pltpu.VMEM)


def far(x):
    return pltpu.with_memory_space_constraint(x, pltpu.HBM)


def dot(a, b, da, db):
    return lax.dot_general(a, b, (((da,), (db,)), ((), ())), preferred_element_type=F32)


def turned(slot, group):
    return (group - slot) & (group - 1)


def place_of(group):
    index = lax.axis_index("seq")
    return index & 1, (index >> 1) & (group - 1)


def partner(core, rank, slot, group):
    return rank ^ (slot + core * (turned(slot, group) - slot))


def away_kernel(q, k, v, g, out, qs, ks, vs, gs, sems, *, part):
    slots = q.shape[0] // 2
    core, rank = place_of(slots)
    core = 1 - core
    copies = []
    for n, (there, here) in enumerate(((k, ks), (v, vs), (q, qs), (g, gs))):
        for m, slot in enumerate(part):
            head = core * slots + partner(core, rank, slot, slots)
            copies.append(pltpu.make_async_copy(there.at[head], here.at[m], sems.at[n, m]))
            copies[-1].start()
    for copy in copies[: 2 * len(part)]:
        copy.wait()
    for m in range(len(part)):
        out[m, 0] = dot(ks[m], vs[m], 0, 0)
    for copy in copies[2 * len(part) :]:
        copy.wait()
    for m in range(len(part)):
        out[m, 1] = dot(qs[m], gs[m], 0, 0)


def near_kernel(q, k, v, g, *outs, parts, other):
    slots = q.shape[0] // 2
    core, rank = place_of(slots)
    core = 1 - core if other else core
    for out, part in zip(outs, parts):
        for m, slot in enumerate(part):
            head = core * slots + partner(core, rank, slot, slots)
            out[m, 0] = dot(k[head], v[head], 0, 0)
            out[m, 1] = dot(q[head], g[head], 0, 0)


def state_call(kernel, data, parts, place, spec, scratch):
    _, tokens, width = data[0].shape
    count = sum(len(part) for part in parts)
    return pl.pallas_call(
        kernel,
        out_shape=[pltpu.VMEM((len(part), 2, width, width), F32) for part in parts],
        in_specs=[spec] * 4,
        out_specs=[WHOLE] * len(parts),
        scratch_shapes=scratch,
        compiler_params=ROOM,
        cost_estimate=pl.CostEstimate(
            flops=count * 4 * tokens * width * width,
            bytes_accessed=count * 8 * tokens * width,
            transcendentals=0,
        ),
    )(*[place(x) for x in data])


def away_states(data, part):
    _, tokens, width = data[0].shape
    scratch = [pltpu.VMEM((len(part), tokens, width), BF16)] * 4
    scratch.append(pltpu.SemaphoreType.DMA((4, len(part))))
    kernel = functools.partial(away_kernel, part=part)
    return state_call(kernel, data, [part], far, FAR, scratch)


def near_states(data, parts, other):
    kernel = functools.partial(near_kernel, parts=parts, other=other)
    return state_call(kernel, data, parts, near, WHOLE, [])


def total_kernel(came, keep, *refs):
    *totals, inner, outer = refs
    core = lax.axis_index("seq") & 1
    for i, out in enumerate(totals):
        out[...] = came[i] + keep[i]
        inner[i] = jnp.where(core == 0, came[i, 1], came[i, 0])
        outer[i] = jnp.where(core == 0, keep[i, 0], keep[i, 1])


def totals_of(came, keep):
    slots, _, width, _ = keep.shape
    return pl.pallas_call(
        total_kernel,
        out_shape=[pltpu.VMEM((2, width, width), F32)] * slots
        + [pltpu.VMEM((slots, width, width), F32)] * 2,
        in_specs=[WHOLE] * 2,
        out_specs=[WHOLE] * (slots + 2),
        compiler_params=ROOM,
    )(near(came), near(keep))


def outside_kernel(carry, *refs, slot, group):
    out = refs[-1]
    core, rank = place_of(group)
    earlier, later = carry[0], carry[1]
    there = partner(core, rank, slot, group)
    for i in range(group):
        if i != slot:
            before = partner(core, rank, i, group) < there
            earlier = earlier + jnp.where(before, refs[i][0], 0.0)
            later = later + jnp.where(before, 0.0, refs[i][1])
    out[0] = earlier
    out[1] = later


def outside_of(carry, held, slot):
    return pl.pallas_call(
        functools.partial(outside_kernel, slot=slot, group=len(held)),
        out_shape=pltpu.VMEM(carry.shape, F32),
        in_specs=[WHOLE] * (1 + len(held)),
        out_specs=WHOLE,
        compiler_params=ROOM,
    )(near(carry), *[near(x) for x in held])


def share_kernel(*refs, rows):
    mine, theirs = refs[-2:]
    first = lax.axis_index("seq") & 1 == 0
    for n, i in enumerate(rows):
        inner, outer, around = refs[3 * n : 3 * n + 3]
        earlier, later = around[0], around[1]
        mine[n, 0] = earlier + jnp.where(first, 0.0, inner[i])
        mine[n, 1] = later + jnp.where(first, inner[i], 0.0)
        theirs[n, 0] = earlier + jnp.where(first, outer[i], 0.0)
        theirs[n, 1] = later + jnp.where(first, 0.0, outer[i])


def shares_of(inner, outer, around, slots, after=()):
    shape = (len(slots), *around[0].shape)
    given = [x for i in slots for x in (inner[i][0], outer[i][0], around[i])]
    return pl.pallas_call(
        functools.partial(share_kernel, rows=[inner[i][1] for i in slots]),
        out_shape=[pltpu.VMEM(shape, F32)] * 2,
        in_specs=[WHOLE] * len(given) + [PLACED] * len(after),
        out_specs=[WHOLE] * 2,
        compiler_params=ROOM,
    )(*[near(x) for x in (*given, *after)])


def local_kernel(qs, ks, vs, gs, after, gq, gk, gv):
    heads, tokens, _ = qs.shape
    row = lax.broadcasted_iota(jnp.int32, (tokens, tokens), 0)
    col = lax.broadcasted_iota(jnp.int32, (tokens, tokens), 1)
    for i in range(heads):
        q, k, v, g = qs[i], ks[i], vs[i], gs[i]
        score = jnp.where(row >= col, dot(g, v, 1, 1), 0.0).astype(BF16)
        gq[i] = dot(score, k, 1, 0)
        score = jnp.where(row <= col, dot(v, g, 1, 1), 0.0).astype(BF16)
        gk[i] = dot(score, q, 1, 0)
        score = jnp.where(row <= col, dot(k, q, 1, 1), 0.0).astype(BF16)
        gv[i] = dot(score, g, 1, 0)


def local_parts(data, after):
    heads, tokens, width = data[0].shape
    return pl.pallas_call(
        local_kernel,
        out_shape=[pltpu.VMEM(data[0].shape, F32)] * 3,
        in_specs=[WHOLE] * 4 + [PLACED],
        out_specs=[WHOLE] * 3,
        compiler_params=ROOM,
        cost_estimate=pl.CostEstimate(
            flops=heads * 12 * tokens * tokens * width,
            bytes_accessed=heads * 20 * tokens * width,
            transcendentals=0,
        ),
    )(*[near(x) for x in data], near(after))


def block_kernel(after, *refs):
    out = refs[-1]
    total = refs[0][...]
    for x in refs[1:-1]:
        total = total + x[...]
    out[...] = total


def block_sum(held, after):
    return pl.pallas_call(
        block_kernel,
        out_shape=pltpu.VMEM(held[0].shape, F32),
        in_specs=[PLACED] + [WHOLE] * len(held),
        out_specs=WHOLE,
        compiler_params=ROOM,
    )(near(after), *[near(x) for x in held])


def final_kernel(k, v, g, lq, lk, lv, *refs, pieces, given):
    bq, bk, bv, sems = refs[-4:]
    gq, gk, gv, *marks = refs[len(pieces) + given : -4]
    for mark in marks:
        mark[...] = jnp.zeros_like(mark)
    half = k.shape[0] // 2
    core, rank = place_of(half)
    copies = []
    for state, (other, slots) in zip(refs, pieces):
        side = 1 - core if other else core
        for i, slot in enumerate(slots):
            earlier, later = state[i, 0].astype(BF16), state[i, 1].astype(BF16)
            head, n = side * half + partner(side, rank, slot, half), len(copies) // 3
            bq[n] = (lq[head] + dot(g[head], earlier, 1, 1)).astype(BF16)
            bk[n] = (lk[head] + dot(v[head], later, 1, 1)).astype(BF16)
            bv[n] = (lv[head] + dot(k[head], later, 1, 0)).astype(BF16)
            for m, (here, there) in enumerate(((bq, gq), (bk, gk), (bv, gv))):
                copies.append(pltpu.make_async_copy(here.at[n], there.at[head], sems.at[n, m]))
                copies[-1].start()
    for copy in copies:
        copy.wait()


def final_sums(data, parts, states, pieces, filled=()):
    _, tokens, width = data[0].shape
    count = sum(len(slots) for _, slots in pieces)
    held = 6 + len(states)
    return pl.pallas_call(
        functools.partial(final_kernel, pieces=pieces, given=len(filled)),
        out_shape=[jax.ShapeDtypeStruct(data[0].shape, BF16)] * 3
        + [pltpu.VMEM((8, width), F32)] * (not filled),
        in_specs=[WHOLE] * held + [PLACED] * len(filled),
        out_specs=[PLACED] * 3 + [WHOLE] * (not filled),
        input_output_aliases={held + n: n for n in range(len(filled))},
        scratch_shapes=[pltpu.VMEM((count, tokens, width), BF16)] * 3
        + [pltpu.SemaphoreType.DMA((count, 3))],
        compiler_params=ROOM,
        cost_estimate=pl.CostEstimate(
            flops=count * 6 * tokens * width * width,
            bytes_accessed=count * 6 * tokens * width,
            transcendentals=0,
        ),
    )(*[near(x) for x in (*data[1:], *parts, *states)], *filled)


def swap(x, mask):
    count = lax.axis_size("seq")
    return lax.ppermute(x, "seq", [(i, i ^ mask) for i in range(count)])


def swap_slot(x, slot, group):
    count = lax.axis_size("seq")
    masks = (2 * slot, 2 * turned(slot, group))
    return lax.ppermute(x, "seq", [(i, i ^ masks[i & 1]) for i in range(count)])


def sliced_body(group):
    def body(queries, key_rows, value_rows, grad_out):
        count, index = lax.axis_size("seq"), lax.axis_index("seq")
        slots = group
        data = (queries, key_rows, value_rows, grad_out)

        split = ((1, 2), (0, *range(3, slots)))
        away = away_states(data, split[0]) + near_states(data, split[1:], True)
        keep = near_states(data, split, False)
        came = [swap(x, 1) for x in away]
        total, inner, outer = {}, {}, {}
        for part, a, b in zip(split, came, keep):
            *sums, into, from_here = totals_of(a, b)
            for n, j in enumerate(part):
                total[j], inner[j], outer[j] = sums[n], (into, n), (from_here, n)

        held = [total[0]] + [swap_slot(total[j], j, group) for j in range(1, group)]
        parts = local_parts(data, total[0])

        block = block_sum(held, parts[0])
        keys, rests = block[0], block[1]
        carry = jnp.zeros_like(block)
        bit = 2 * group
        while bit < count:
            upper = (index & bit) != 0
            if 2 * bit < count:
                got = swap(jnp.stack([keys, rests]), bit)
                keys, rests = keys + got[0], rests + got[1]
                got_keys, got_rests = got[0], got[1]
            else:
                got_keys = got_rests = swap(jnp.where(upper, rests, keys), bit)
            carry = carry + jnp.stack(
                [jnp.where(upper, got_keys, 0.0), jnp.where(upper, 0.0, got_rests)]
            )
            bit *= 2

        around = [outside_of(carry, held, j) for j in range(group)]
        around = [swap_slot(x, j, group) if j else x for j, x in enumerate(around)]
        soon, late = (0, group - 1), tuple(range(group - 2, 0, -1))
        mine, theirs = shares_of(inner, outer, around, soon)
        other = swap(theirs, 1)
        *done, mark = final_sums(data, parts, [mine], [(False, soon)])
        late_mine, late_theirs = shares_of(inner, outer, around, late, [mark])
        late_other = swap(late_theirs, 1)
        pieces = [(True, soon), (False, late)]
        done = final_sums(data, parts, [other, late_mine], pieces, done)
        return tuple(final_sums(data, parts, [late_other], [(True, late)], done))

    return body


def solution(mesh):
    count = mesh.shape["seq"]

    def run(queries, key_rows, value_rows, grad_out):
        heads = queries.shape[0] // mesh.shape["head"]
        tokens = queries.shape[1] // count
        group = heads // 2
        powers = all(n > 0 and n & (n - 1) == 0 for n in (count, group))
        fits = powers and heads == 2 * group and group >= 4 and tokens == TILE and count >= 4 * group
        body = sliced_body(group) if fits else plain_body
        return jax.shard_map(
            body, mesh=mesh, in_specs=(SPEC,) * 4, out_specs=(SPEC,) * 3, check_vma=False
        )(queries, key_rows, value_rows, grad_out)

    return run
```
